512 devices in a mesh: rows: 128 (over z, y, core), grp: 4 (over x).
Axes of the slice: x: 4, y: 8, z: 8, core: 2. Of those that a mesh axis runs over, the one named last changes fastest.
Arguments:
- owner: int32 [16384, 24, 3], P('rows', 'grp'), may hold values from 0 to 127, as said below
- offset: int32 [16384, 24, 3], P('rows', 'grp'), may hold values from 0 to 511
- tables: float32 [12, 65536, 128], P('grp', 'rows'), may hold values from -6 to 6
- w_first: bfloat16 [3072, 1024], P('grp'), may hold values from -0.109375 to 0.109375
- b_first: float32 [1024], replicated, may hold values from -3 to 3
- w_out: float32 [1024], replicated, may hold values from -0.1875 to 0.1875
- labels: int32 [16384], P('rows'), may hold values 0 or 1
Outputs:
- table_grad: float32 [12, 65536, 128], P('grp', 'rows')
- losses: float32 [16384], P(('rows', 'grp'))
The draws below stay inside these ranges and needn't reach their ends.
Inputs may be any that keep to these rules, and one draw needn't show every extreme that they name: Of the lookups of one device (its 128 samples and 6 features, all three hashes) at most 72 name one owner, and in every draw some owner gets exactly 72. Among the lookups of one device to one owner for one table, at most 8 distinct offsets occur, and that bound is reached in every draw.
All inputs are finite; a program needn't handle non-finite values. No bound on the sum of `labels` on one device may be relied on, other than what follows from the above.
Results may differ from the reference program's by a relative error of at most 0.005.
Values may be sent and summed in bfloat16 or wider, within the bound.
No kernel may reach another device: no remote copies, remote signals or barrier semaphores. Data moves between devices by JAX's collectives and lax.ppermute only.
A program may use at most 64 MiB of HBM per device.

```python
import jax
import jax.numpy as jnp
from jax import lax

E = 128
H = 1024
F_GRP = 6
B_DEV = 128
ROWS_DEV = 512
BATCH = 16384
FEATURES = 24
TAB_ROWS = 65536
HOTK = 24
UNIQ = 8
N_GRP = 4


def layout_pair(key):
    row_devices = BATCH // B_DEV
    group_devices = FEATURES // F_GRP
    block_size = B_DEV * F_GRP
    base_key = jax.random.fold_in(key, 7001)

    def device_block(block_key):
        subkeys = jax.random.split(block_key, 4)
        hot_owner = jax.random.randint(subkeys[0], (), 0, row_devices)
        rank_of = jnp.stack([jax.random.permutation(jax.random.fold_in(subkeys[1], column), block_size) for column in range(3)], axis=1).astype(jnp.int32)
        spread_owner = (hot_owner + 1 + (rank_of - HOTK) % (row_devices - 1)) % row_devices
        owners = jnp.where(rank_of < HOTK, hot_owner, spread_owner).astype(jnp.int32)
        pool_pick = jnp.where(rank_of < HOTK, rank_of % UNIQ, jax.random.randint(subkeys[2], (block_size, 3), 0, UNIQ))
        pool_base = jax.random.randint(subkeys[3], (row_devices, 3), 0, ROWS_DEV)
        pool_step = ROWS_DEV // UNIQ
        chosen_base = pool_base[owners, jnp.arange(3, dtype=jnp.int32)[None, :]]
        offsets = (chosen_base + pool_pick * pool_step) % ROWS_DEV
        return (owners.reshape(B_DEV, F_GRP, 3), offsets.astype(jnp.int32).reshape(B_DEV, F_GRP, 3))
    block_keys = jax.random.split(base_key, row_devices * group_devices)
    owners, offsets = jax.vmap(device_block)(block_keys)
    owners = owners.reshape(row_devices, group_devices, B_DEV, F_GRP, 3).transpose(0, 2, 1, 3, 4).reshape(BATCH, FEATURES, 3)
    offsets = offsets.reshape(row_devices, group_devices, B_DEV, F_GRP, 3).transpose(0, 2, 1, 3, 4).reshape(BATCH, FEATURES, 3)
    return (owners, offsets)


def draw_owner(key, part):
    return layout_pair(key)[0]


def draw_offset(key, part):
    return layout_pair(key)[1]


def place_ends(result, stream_key, least, top_value):
    longest = result.shape.index(max(result.shape))
    spots = []
    for shift in (0, 1):
        where = [jax.random.randint(jax.random.fold_in(stream_key, axis), (), 0, length) for axis, length in enumerate(result.shape)]
        where[longest] = (where[longest] + shift) % result.shape[longest]
        spots.append(tuple(where))
    return result.at[spots[0]].set(least).at[spots[1]].set(top_value)


def levels(rng, dims, cuts, low, largest):
    def one(dim, parts):
        draws = jax.random.uniform(jax.random.fold_in(jax.random.fold_in(rng, 6), dim), (parts,), jnp.float32, low / len(cuts), largest / len(cuts))
        return jnp.repeat(jnp.exp(draws), dims[dim] // parts).reshape((-1,) + (1,) * (len(dims) - dim - 1))

    level = one(*cuts[0])
    for cut in cuts[1:]:
        level = level * one(*cut)
    return level


def normal_values(key, shape, scale, limit, cuts=(), kind=jnp.bfloat16):
    values = jax.random.normal(key, shape, jnp.float32) * scale
    if len(cuts) > 0:
        values = levels(key, shape, cuts, -0.22, 0.18) * values
    return jnp.clip(values, min=-limit, max=limit).astype(kind)


def setup_inputs(seed: int = 0) -> dict:
    key_of = jax.random.split(jax.random.key(seed), 8)
    return {
        "owner": draw_owner(jax.random.fold_in(key_of[7], 71), 0),
        "offset": draw_offset(jax.random.fold_in(key_of[7], 71), 0),
        "tables": normal_values(key_of[2], (3 * N_GRP, TAB_ROWS, E), 1.0, 6.0, ((0, 4), (1, 128)), jnp.float32),
        "w_first": normal_values(key_of[3], (FEATURES * E, H), (FEATURES * E) ** -0.5, 0.109375, ((0, 4),)),
        "b_first": normal_values(key_of[4], (H,), 0.5, 3.0, (), jnp.float32),
        "w_out": normal_values(key_of[5], (H,), H ** -0.5, 0.1875, (), jnp.float32),
        "labels": place_ends((jax.random.randint(key_of[6], (BATCH,), 0, 2) < 1).astype(jnp.int32), jax.random.fold_in(key_of[6], 1), 0, 1),
    }


def reference(owner, offset, tables, w_first, b_first, w_out, labels):
    table_kind = jnp.arange(3, dtype=jnp.int32)
    feature_group = jnp.arange(FEATURES, dtype=jnp.int32) // F_GRP
    table_id = jnp.broadcast_to(feature_group[None, :, None] * 3 + table_kind[None, None, :], owner.shape).astype(jnp.int32)
    row_id = (owner * ROWS_DEV + offset).astype(jnp.int32)
    looked_low = tables[table_id, row_id].astype(jnp.bfloat16)
    looked = lax.optimization_barrier(looked_low).astype(jnp.float32)
    embedded = looked[:, :, 0] * looked[:, :, 1] + looked[:, :, 2]
    features = embedded.reshape(BATCH, FEATURES * E).astype(jnp.bfloat16)
    pre_act = jnp.dot(features, w_first, preferred_element_type=jnp.float32) + b_first
    gate_sig = jax.nn.sigmoid(pre_act)
    logits = jnp.sum(pre_act * gate_sig * w_out, axis=1)
    targets = labels.astype(jnp.float32)
    losses = jax.nn.softplus(logits) - targets * logits
    grad_logit = jax.nn.sigmoid(logits) - targets
    grad_pre = (grad_logit[:, None] * w_out * (gate_sig * (1.0 + pre_act * (1.0 - gate_sig)))).astype(jnp.bfloat16)
    grad_emb = jnp.dot(grad_pre, w_first.T, preferred_element_type=jnp.float32).reshape(BATCH, FEATURES, E)
    row_grads = jnp.stack([grad_emb * looked[:, :, 1], grad_emb * looked[:, :, 0], grad_emb], axis=2)
    table_grad = jnp.zeros((3 * N_GRP, TAB_ROWS, E), jnp.float32).at[table_id, row_id].add(row_grads)
    return table_grad, losses
```

```python
import functools

import jax
import jax.numpy as jnp
from jax import lax
from jax.experimental import pallas as pl
from jax.experimental.pallas import tpu as pltpu
from jax.sharding import PartitionSpec as P

SLOTS = 8
LANES = 128
VMEM = 40 * 2**20
BF16 = jnp.bfloat16
F32 = jnp.float32


def dot(a, b, ca, cb):
    return lax.dot_general(a, b, (((ca,), (cb,)), ((), ())), preferred_element_type=F32)


def iota(shape, dim):
    return lax.broadcasted_iota(jnp.int32, shape, dim)


def hot(mask):
    return jnp.where(mask, 1.0, 0.0).astype(BF16)


def call(kernel, out_shape, flops=0, n_in=1, scalars=()):
    specs = [
        pl.BlockSpec(memory_space=pltpu.SMEM if i in scalars else pltpu.VMEM) for i in range(n_in)
    ]
    return pl.pallas_call(
        kernel,
        out_shape=out_shape,
        in_specs=specs,
        compiler_params=pltpu.CompilerParams(vmem_limit_bytes=VMEM),
        cost_estimate=pl.CostEstimate(flops=flops, bytes_accessed=2**20, transcendentals=0),
    )


def index_kernel(rows_dev, codes_ref, cols_ref, out_ref):
    n_owner = out_ref.shape[0]
    n_look = codes_ref.shape[1]
    before = hot(iota((rows_dev, rows_dev), 0) < iota((rows_dev, rows_dev), 1))
    offsets = iota((n_owner, rows_dev), 1)
    lane = iota((n_owner, LANES), 1)
    asked = jnp.full((n_owner, LANES), -1, jnp.int32)
    for k in range(3):
        code = codes_ref[k : k + 1, :]
        owner = code // rows_dev
        offset = code - owner * rows_dev
        owner_hot = hot(iota((n_owner, n_look), 0) == owner)
        offset_hot = hot(iota((rows_dev, n_look), 0) == offset)
        present = dot(owner_hot, offset_hot, 1, 1) > 0.5
        rank = dot(hot(present), before, 1, 0)
        at_owner = dot(rank.astype(BF16), offset_hot, 1, 0)
        slot = jnp.sum(owner_hot.astype(F32) * at_owner, axis=0, keepdims=True)
        cols_ref[k : k + 1, :] = owner * SLOTS + slot.astype(jnp.int32)
        rank = jnp.where(present, rank.astype(jnp.int32), -1)
        for s in range(SLOTS):
            found = jnp.where(rank == s, offsets + 1, 0).astype(F32)
            found = jnp.sum(found, axis=1, keepdims=True).astype(jnp.int32) - 1
            asked = jnp.where(lane == k * SLOTS + s, found, asked)
    out_ref[...] = asked


def request_column(codes, k):
    n_src = codes.shape[0]
    wide = jnp.broadcast_to(codes[:, None, :].astype(F32), (n_src, SLOTS, LANES))
    mine = iota((1, SLOTS, LANES), 2) == iota((1, SLOTS, LANES), 1) + k * SLOTS
    column = jnp.sum(jnp.where(mine, wide, 0.0), axis=2, keepdims=True)
    return column.reshape(n_src * SLOTS, 1).astype(jnp.int32)


def fetch_kernel(codes_ref, table_ref, out_ref):
    n_src = codes_ref.shape[0]
    rows_dev = table_ref.shape[1]
    width = table_ref.shape[2]
    codes = codes_ref[...]
    parts = []
    for k in range(3):
        onehot = hot(iota((n_src * SLOTS, rows_dev), 1) == request_column(codes, k))
        rows = dot(onehot, table_ref[k].astype(BF16), 1, 0)
        parts.append(rows.reshape(n_src, SLOTS, width))
    rows = jnp.concatenate(parts, axis=1)
    out_ref[...] = rows.reshape(n_src * 3 * SLOTS, width).astype(BF16)


def forward_kernel(rows_ref, cols_ref, w_ref, pre_ref, looked_ref):
    width = rows_ref.shape[1]
    n_look = cols_ref.shape[1]
    n_owner = rows_ref.shape[0] // (3 * SLOTS)
    n_feat = w_ref.shape[0] // width
    rows = rows_ref[...].astype(F32).reshape(n_owner, 3 * SLOTS, width)
    looked = []
    for k in range(3):
        mine = rows[:, k * SLOTS : (k + 1) * SLOTS, :].reshape(n_owner * SLOTS, width).astype(BF16)
        onehot = hot(iota((n_owner * SLOTS, n_look), 0) == cols_ref[k : k + 1, :])
        looked.append(dot(mine, onehot, 0, 0))
    looked_ref[0] = looked[0].astype(BF16)
    looked_ref[1] = looked[1].astype(BF16)
    emb = (looked[0] * looked[1] + looked[2]).astype(BF16)
    n_b = n_look // n_feat
    emb = jnp.concatenate([emb[:, f * n_b : (f + 1) * n_b] for f in range(n_feat)], axis=0)
    pre_ref[...] = dot(emb, w_ref[...], 0, 0).astype(BF16)


def head_kernel(grp_ref, pre_ref, b_ref, w_out_ref, labels_ref, grad_ref, loss_ref):
    n_grp, share, _ = grad_ref.shape
    pre = b_ref[...]
    for g in range(n_grp):
        pre = pre + pre_ref[g * share : (g + 1) * share, :].astype(F32)
    w_out = w_out_ref[...]
    sig = jax.nn.sigmoid(pre)
    logits = jnp.sum(pre * sig * w_out, axis=1, keepdims=True)
    n_b = labels_ref.shape[1]
    mine = iota((share, n_b), 1) == iota((share, n_b), 0) + grp_ref[0] * share
    targets = jnp.sum(jnp.where(mine, labels_ref[...].astype(F32), 0.0), axis=1, keepdims=True)
    soft = jnp.maximum(logits, 0.0) + jnp.log1p(jnp.exp(-jnp.abs(logits)))
    losses = soft - targets * logits
    grad_logit = jax.nn.sigmoid(logits) - targets
    grad = (grad_logit * w_out * (sig * (1.0 + pre * (1.0 - sig)))).astype(BF16)
    for g in range(n_grp):
        grad_ref[g] = grad
    diagonal = iota((share, share), 0) == iota((share, share), 1)
    loss_ref[...] = jnp.sum(jnp.where(diagonal, losses, 0.0), axis=0, keepdims=True)


def backward_kernel(grad_ref, w_ref, cols_ref, looked_ref, out_ref):
    width = out_ref.shape[1]
    n_look = cols_ref.shape[1]
    n_owner = out_ref.shape[0] // (3 * SLOTS)
    n_feat = w_ref.shape[0] // width
    grad_t = dot(w_ref[...], grad_ref[...], 1, 1)
    emb_t = jnp.concatenate([grad_t[f * width : (f + 1) * width] for f in range(n_feat)], axis=1)
    factors = (looked_ref[1].astype(F32), looked_ref[0].astype(F32), None)
    parts = []
    for k in range(3):
        row_t = emb_t if factors[k] is None else emb_t * factors[k]
        high = row_t.astype(BF16)
        low = (row_t - high.astype(F32)).astype(BF16)
        onehot = hot(iota((n_owner * SLOTS, n_look), 0) == cols_ref[k : k + 1, :])
        sums = dot(onehot, jnp.concatenate([high, low], axis=0), 1, 1)
        sums = sums[:, :width] + sums[:, width:]
        parts.append(sums.reshape(n_owner, SLOTS, width))
    out_ref[...] = jnp.concatenate(parts, axis=1).reshape(n_owner * 3 * SLOTS, width).astype(BF16)


def owner_kernel(codes_ref, grads_ref, out_ref):
    n_src = codes_ref.shape[0]
    rows_dev, width = out_ref.shape[1:]
    codes = codes_ref[...]
    grads = grads_ref[...].astype(F32).reshape(n_src, 3 * SLOTS, width)
    for k in range(3):
        mine = grads[:, k * SLOTS : (k + 1) * SLOTS, :].reshape(n_src * SLOTS, width).astype(BF16)
        onehot = hot(iota((n_src * SLOTS, rows_dev), 1) == request_column(codes, k))
        out_ref[k] = dot(mine, onehot, 0, 0).T


def exchange(array, axis):
    return lax.all_to_all(array, axis, split_axis=0, concat_axis=0, tiled=True)


def body(owner, offset, tables, w_first, b_first, w_out, labels):
    n_rows = lax.axis_size("rows")
    n_grp = lax.axis_size("grp")
    n_b, n_feat = owner.shape[:2]
    rows_dev, width = tables.shape[1:]
    hidden = w_first.shape[1]
    n_look = n_b * n_feat
    shape = jax.ShapeDtypeStruct
    codes = (owner * rows_dev + offset).transpose(2, 1, 0).reshape(3, n_look)
    cols, asked = call(
        functools.partial(index_kernel, rows_dev),
        (shape((3, n_look), jnp.int32), shape((n_rows, LANES), jnp.int32)),
    )(codes)
    requests = exchange(asked, "rows")
    rows = call(fetch_kernel, shape((n_rows * 3 * SLOTS, width), BF16), n_in=2)(requests, tables)
    rows = exchange(rows, "rows")
    pre, looked = call(
        forward_kernel,
        (shape((n_b, hidden), BF16), shape((2, width, n_look), BF16)),
        n_in=3,
    )(rows, cols, w_first)
    pre = exchange(pre, "grp")
    grp = lax.axis_index("grp").astype(jnp.int32).reshape(1)
    share = n_b // n_grp
    grad, losses = call(
        head_kernel,
        (shape((n_grp, share, hidden), BF16), shape((1, share), F32)),
        n_in=5,
        scalars=(0,),
    )(grp, pre, b_first.reshape(1, hidden), w_out.reshape(1, hidden), labels.reshape(1, n_b))
    grad = exchange(grad.reshape(n_b, hidden), "grp")
    sums = call(backward_kernel, shape((n_rows * 3 * SLOTS, width), BF16), n_in=4)(
        grad, w_first, cols, looked
    )
    sums = exchange(sums, "rows")
    table_grad = call(owner_kernel, shape((3, rows_dev, width), F32), n_in=2)(requests, sums)
    return table_grad, losses.reshape(share)


def solution(mesh):
    placed = (
        P("rows", "grp", None),
        P("rows", "grp", None),
        P("grp", "rows", None),
        P("grp", None),
        P(),
        P(),
        P("rows"),
    )
    return jax.shard_map(
        body,
        mesh=mesh,
        in_specs=placed,
        out_specs=(P("grp", "rows", None), P(("rows", "grp"))),
        check_vma=False,
    )
```

```python
import functools

import jax
import jax.numpy as jnp
from jax import lax
from jax.experimental import pallas as pl
from jax.experimental.pallas import tpu as pltpu
from jax.sharding import PartitionSpec as P

SLOTS = 8
LANES = 128
VMEM = 40 * 2**20
BF16 = jnp.bfloat16
F32 = jnp.float32


def dot(a, b, ca, cb):
    return lax.dot_general(a, b, (((ca,), (cb,)), ((), ())), preferred_element_type=F32)


def iota(shape, dim):
    return lax.broadcasted_iota(jnp.int32, shape, dim)


def hot(mask):
    return jnp.where(mask, 1.0, 0.0).astype(BF16)


def call(kernel, out_shape, flops=0, n_in=1, scalars=()):
    specs = [
        pl.BlockSpec(memory_space=pltpu.SMEM if i in scalars else pltpu.VMEM) for i in range(n_in)
    ]
    return pl.pallas_call(
        kernel,
        out_shape=out_shape,
        in_specs=specs,
        compiler_params=pltpu.CompilerParams(vmem_limit_bytes=VMEM),
        cost_estimate=pl.CostEstimate(flops=flops, bytes_accessed=2**20, transcendentals=0),
    )


def index_kernel(rows_dev, owner_ref, offset_ref, cols_ref, out_ref):
    n_owner = out_ref.shape[0]
    n_look = cols_ref.shape[1]
    n_feat = owner_ref.shape[0]
    before = hot(iota((rows_dev, rows_dev), 0) < iota((rows_dev, rows_dev), 1))
    offsets = iota((n_owner, rows_dev), 1)
    lane = iota((n_owner, LANES), 1)
    asked = jnp.full((n_owner, LANES), -1, jnp.int32)
    for k in range(3):
        owner = jnp.concatenate([owner_ref[f, k : k + 1, :] for f in range(n_feat)], axis=1)
        offset = jnp.concatenate([offset_ref[f, k : k + 1, :] for f in range(n_feat)], axis=1)
        owner_hot = hot(iota((n_owner, n_look), 0) == owner)
        offset_hot = hot(iota((rows_dev, n_look), 0) == offset)
        present = dot(owner_hot, offset_hot, 1, 1) > 0.5
        rank = dot(hot(present), before, 1, 0)
        at_owner = dot(rank.astype(BF16), offset_hot, 1, 0)
        slot = jnp.sum(owner_hot.astype(F32) * at_owner, axis=0, keepdims=True)
        cols_ref[k : k + 1, :] = owner * SLOTS + slot.astype(jnp.int32)
        rank = jnp.where(present, rank.astype(jnp.int32), -1)
        for s in range(SLOTS):
            found = jnp.where(rank == s, offsets + 1, 0).astype(F32)
            found = jnp.sum(found, axis=1, keepdims=True).astype(jnp.int32) - 1
            asked = jnp.where(lane == k * SLOTS + s, found, asked)
    out_ref[...] = asked


def request_column(codes, k):
    n_src = codes.shape[0]
    wide = jnp.broadcast_to(codes[:, None, :].astype(F32), (n_src, SLOTS, LANES))
    mine = iota((1, SLOTS, LANES), 2) == iota((1, SLOTS, LANES), 1) + k * SLOTS
    column = jnp.sum(jnp.where(mine, wide, 0.0), axis=2, keepdims=True)
    return column.reshape(n_src * SLOTS, 1).astype(jnp.int32)


def fetch_kernel(codes_ref, table_ref, out_ref):
    n_src = codes_ref.shape[0]
    rows_dev = table_ref.shape[1]
    width = table_ref.shape[2]
    codes = codes_ref[...]
    parts = []
    for k in range(3):
        onehot = hot(iota((n_src * SLOTS, rows_dev), 1) == request_column(codes, k))
        rows = dot(onehot, table_ref[k].astype(BF16), 1, 0)
        parts.append(rows.reshape(n_src, SLOTS, width))
    rows = jnp.concatenate(parts, axis=1)
    out_ref[...] = rows.reshape(n_src * 3 * SLOTS, width).astype(BF16)


def forward_kernel(rows_ref, cols_ref, w_ref, pre_ref, looked_ref):
    width = rows_ref.shape[1]
    n_look = cols_ref.shape[1]
    n_owner = rows_ref.shape[0] // (3 * SLOTS)
    n_feat = w_ref.shape[0] // width
    rows = rows_ref[...].astype(F32).reshape(n_owner, 3 * SLOTS, width)
    looked = []
    for k in range(3):
        mine = rows[:, k * SLOTS : (k + 1) * SLOTS, :].reshape(n_owner * SLOTS, width).astype(BF16)
        onehot = hot(iota((n_owner * SLOTS, n_look), 0) == cols_ref[k : k + 1, :])
        looked.append(dot(mine, onehot, 0, 0))
    looked_ref[0] = looked[0].astype(BF16)
    looked_ref[1] = looked[1].astype(BF16)
    emb = (looked[0] * looked[1] + looked[2]).astype(BF16)
    n_b = n_look // n_feat
    emb = jnp.concatenate([emb[:, f * n_b : (f + 1) * n_b] for f in range(n_feat)], axis=0)
    pre = dot(emb, w_ref[...], 0, 0).astype(BF16)
    for g in range(pre_ref.shape[0]):
        pre_ref[g] = pre


def backward_kernel(
    grp_ref, pre_ref, b_ref, w_out_ref, labels_ref, w_ref, cols_ref, looked_ref, out_ref, loss_ref
):
    n_grp, n_b, _ = pre_ref.shape
    pre = b_ref[...]
    for g in range(n_grp):
        pre = pre + pre_ref[g].astype(F32)
    w_out = w_out_ref[...]
    sig = jax.nn.sigmoid(pre)
    logits = jnp.sum(pre * sig * w_out, axis=1, keepdims=True)
    diagonal = iota((n_b, n_b), 0) == iota((n_b, n_b), 1)
    targets = jnp.sum(jnp.where(diagonal, labels_ref[...].astype(F32), 0.0), axis=1, keepdims=True)
    soft = jnp.maximum(logits, 0.0) + jnp.log1p(jnp.exp(-jnp.abs(logits)))
    losses = soft - targets * logits
    share = loss_ref.shape[1]
    mine = iota((n_b, share), 0) == iota((n_b, share), 1) + grp_ref[0] * share
    loss_ref[...] = jnp.sum(jnp.where(mine, losses, 0.0), axis=0, keepdims=True)
    grad_logit = jax.nn.sigmoid(logits) - targets
    grad = (grad_logit * w_out * (sig * (1.0 + pre * (1.0 - sig)))).astype(BF16)

    width = out_ref.shape[1]
    n_look = cols_ref.shape[1]
    n_owner = out_ref.shape[0] // (3 * SLOTS)
    n_feat = w_ref.shape[0] // width
    grad_t = dot(w_ref[...], grad, 1, 1)
    emb_t = jnp.concatenate([grad_t[f * width : (f + 1) * width] for f in range(n_feat)], axis=1)
    factors = (looked_ref[1].astype(F32), looked_ref[0].astype(F32), None)
    parts = []
    for k in range(3):
        row_t = emb_t if factors[k] is None else emb_t * factors[k]
        high = row_t.astype(BF16)
        low = (row_t - high.astype(F32)).astype(BF16)
        onehot = hot(iota((n_owner * SLOTS, n_look), 0) == cols_ref[k : k + 1, :])
        sums = dot(onehot, jnp.concatenate([high, low], axis=0), 1, 1)
        sums = sums[:, :width] + sums[:, width:]
        parts.append(sums.reshape(n_owner, SLOTS, width))
    out_ref[...] = jnp.concatenate(parts, axis=1).reshape(n_owner * 3 * SLOTS, width).astype(BF16)


def owner_kernel(codes_ref, grads_ref, out_ref):
    n_src = codes_ref.shape[0]
    rows_dev, width = out_ref.shape[1:]
    codes = codes_ref[...]
    grads = grads_ref[...].astype(F32).reshape(n_src, 3 * SLOTS, width)
    for k in range(3):
        mine = grads[:, k * SLOTS : (k + 1) * SLOTS, :].reshape(n_src * SLOTS, width).astype(BF16)
        onehot = hot(iota((n_src * SLOTS, rows_dev), 1) == request_column(codes, k))
        out_ref[k] = dot(mine, onehot, 0, 0).T


def exchange(array, axis):
    return lax.all_to_all(array, axis, split_axis=0, concat_axis=0, tiled=True)


def body(owner, offset, tables, w_first, b_first, w_out, labels):
    n_rows = lax.axis_size("rows")
    n_grp = lax.axis_size("grp")
    n_b, n_feat = owner.shape[:2]
    rows_dev, width = tables.shape[1:]
    hidden = w_first.shape[1]
    n_look = n_b * n_feat
    shape = jax.ShapeDtypeStruct
    cols, asked = call(
        functools.partial(index_kernel, rows_dev),
        (shape((3, n_look), jnp.int32), shape((n_rows, LANES), jnp.int32)),
        n_in=2,
    )(owner.transpose(1, 2, 0), offset.transpose(1, 2, 0))
    requests = exchange(asked, "rows")
    rows = call(fetch_kernel, shape((n_rows * 3 * SLOTS, width), BF16), n_in=2)(requests, tables)
    rows = exchange(rows, "rows")
    pre, looked = call(
        forward_kernel,
        (shape((n_grp, n_b, hidden), BF16), shape((2, width, n_look), BF16)),
        n_in=3,
    )(rows, cols, w_first)
    pre = exchange(pre, "grp")
    grp = lax.axis_index("grp").astype(jnp.int32).reshape(1)
    share = n_b // n_grp
    sums, losses = call(
        backward_kernel,
        (shape((n_rows * 3 * SLOTS, width), BF16), shape((1, share), F32)),
        n_in=8,
        scalars=(0,),
    )(
        grp,
        pre,
        b_first.reshape(1, hidden),
        w_out.reshape(1, hidden),
        labels.reshape(1, n_b),
        w_first,
        cols,
        looked,
    )
    sums = exchange(sums, "rows")
    table_grad = call(owner_kernel, shape((3, rows_dev, width), F32), n_in=2)(requests, sums)
    return table_grad, losses.reshape(share)


def solution(mesh):
    placed = (
        P("rows", "grp", None),
        P("rows", "grp", None),
        P("grp", "rows", None),
        P("grp", None),
        P(),
        P(),
        P("rows"),
    )
    return jax.shard_map(
        body,
        mesh=mesh,
        in_specs=placed,
        out_specs=(P("grp", "rows", None), P(("rows", "grp"))),
        check_vma=False,
    )
```

```python
import jax
import jax.numpy as jnp
from jax import lax
from jax.experimental import pallas as pl
from jax.experimental.pallas import tpu as pltpu
from jax.sharding import PartitionSpec as P

SLOTS = 8
LANES = 128
VMEM = 40 * 2**20
VMEM_INDEX = 55_750_000
BF16 = jnp.bfloat16
F32 = jnp.float32


def dot(a, b, ca, cb):
    return lax.dot_general(a, b, (((ca,), (cb,)), ((), ())), preferred_element_type=F32)


def iota(shape, dim):
    return lax.broadcasted_iota(jnp.int32, shape, dim)


def hot(mask):
    return jnp.where(mask, 1.0, 0.0).astype(BF16)


def call(kernel, out_shape, n_in=1, spaces=None, scratch=(), vmem=VMEM, flops=0):
    spaces = spaces or [pltpu.VMEM] * n_in
    return pl.pallas_call(
        kernel,
        out_shape=out_shape,
        in_specs=[pl.BlockSpec(memory_space=space) for space in spaces],
        scratch_shapes=scratch,
        compiler_params=pltpu.CompilerParams(vmem_limit_bytes=vmem),
        cost_estimate=pl.CostEstimate(flops=flops, bytes_accessed=2**20, transcendentals=0),
    )


def index_kernel(
    codes_ref,
    table_hbm,
    grp_ref,
    cols_ref,
    out_ref,
    low_ref,
    table_ref,
    sem,
):
    copy = pltpu.make_async_copy(table_hbm, table_ref, sem)
    copy.start()
    rows_dev = table_ref.shape[1]
    n_owner = out_ref.shape[0]
    n_look = cols_ref.shape[1]
    n_feat = codes_ref.shape[0]
    before = hot(iota((rows_dev, rows_dev), 0) < iota((rows_dev, rows_dev), 1))
    offsets = iota((n_owner, rows_dev), 1)
    lane = iota((n_owner, LANES), 1)
    asked = jnp.full((n_owner, LANES), -1, jnp.int32)
    for k in range(3):
        code = jnp.concatenate([codes_ref[f, k : k + 1, :] for f in range(n_feat)], axis=1)
        owner = code // rows_dev
        offset = code - owner * rows_dev
        owner_hot = hot(iota((n_owner, n_look), 0) == owner)
        offset_hot = hot(iota((rows_dev, n_look), 0) == offset)
        present = dot(owner_hot, offset_hot, 1, 1) > 0.5
        rank = dot(hot(present), before, 1, 0)
        at_owner = dot(rank.astype(BF16), offset_hot, 1, 0)
        slot = jnp.sum(owner_hot.astype(F32) * at_owner, axis=0, keepdims=True)
        cols_ref[k : k + 1, :] = owner * SLOTS + slot.astype(jnp.int32)
        rank = jnp.where(present, rank.astype(jnp.int32), -1)
        for s in range(SLOTS):
            found = jnp.where(rank == s, offsets + 1, 0).astype(F32)
            found = jnp.sum(found, axis=1, keepdims=True).astype(jnp.int32) - 1
            asked = jnp.where(lane == k * SLOTS + s, found, asked)
    out_ref[...] = asked
    cols_ref[3:4, :] = jnp.full((1, n_look), grp_ref[0], jnp.int32)
    copy.wait()
    low_ref[...] = table_ref[...].astype(BF16)


def request_column(codes, k):
    n_src = codes.shape[0]
    wide = jnp.broadcast_to(codes[:, None, :].astype(F32), (n_src, SLOTS, LANES))
    mine = iota((1, SLOTS, LANES), 2) == iota((1, SLOTS, LANES), 1) + k * SLOTS
    column = jnp.sum(jnp.where(mine, wide, 0.0), axis=2, keepdims=True)
    return column.reshape(n_src * SLOTS, 1).astype(jnp.int32)


def fetch_kernel(codes_ref, table_ref, out_ref):
    n_src = codes_ref.shape[0]
    rows_dev = table_ref.shape[1]
    width = table_ref.shape[2]
    codes = codes_ref[...]
    parts = []
    for k in range(3):
        onehot = hot(iota((n_src * SLOTS, rows_dev), 1) == request_column(codes, k))
        rows = dot(onehot, table_ref[k], 1, 0)
        parts.append(rows.reshape(n_src, SLOTS, width))
    rows = jnp.concatenate(parts, axis=1)
    out_ref[...] = rows.reshape(n_src * 3 * SLOTS, width).astype(BF16)


def forward_kernel(rows_ref, cols_ref, w_ref, pre_ref, looked_ref):
    width = rows_ref.shape[1]
    n_look = cols_ref.shape[1]
    n_owner = rows_ref.shape[0] // (3 * SLOTS)
    n_feat = w_ref.shape[0] // width
    rows = rows_ref[...].astype(F32).reshape(n_owner, 3 * SLOTS, width)
    looked = []
    for k in range(3):
        mine = rows[:, k * SLOTS : (k + 1) * SLOTS, :].reshape(n_owner * SLOTS, width).astype(BF16)
        onehot = hot(iota((n_owner * SLOTS, n_look), 0) == cols_ref[k : k + 1, :])
        looked.append(dot(mine, onehot, 0, 0))
    looked_ref[0] = looked[0].astype(BF16)
    looked_ref[1] = looked[1].astype(BF16)
    emb = (looked[0] * looked[1] + looked[2]).astype(BF16)
    n_b = n_look // n_feat
    emb = jnp.concatenate([emb[:, f * n_b : (f + 1) * n_b] for f in range(n_feat)], axis=0)
    pre = dot(emb, w_ref[...], 0, 0).astype(BF16)
    for g in range(pre_ref.shape[0]):
        pre_ref[g] = pre


def backward_kernel(
    pre_ref, b_ref, w_out_ref, labels_ref, w_ref, cols_ref, looked_ref, out_ref, loss_ref
):
    n_grp, n_b, _ = pre_ref.shape
    pre = b_ref[...]
    for g in range(n_grp):
        pre = pre + pre_ref[g].astype(F32)
    w_out = w_out_ref[...]
    sig = jax.nn.sigmoid(pre)
    logits = jnp.sum(pre * sig * w_out, axis=1, keepdims=True)
    diagonal = iota((n_b, n_b), 0) == iota((n_b, n_b), 1)
    targets = jnp.sum(jnp.where(diagonal, labels_ref[...].astype(F32), 0.0), axis=1, keepdims=True)
    soft = jnp.maximum(logits, 0.0) + jnp.log1p(jnp.exp(-jnp.abs(logits)))
    losses = soft - targets * logits
    share = loss_ref.shape[1]
    mine = iota((n_b, share), 0) == iota((n_b, share), 1) + cols_ref[3:4, :share] * share
    loss_ref[...] = jnp.sum(jnp.where(mine, losses, 0.0), axis=0, keepdims=True)
    grad_logit = jax.nn.sigmoid(logits) - targets
    grad = (grad_logit * w_out * (sig * (1.0 + pre * (1.0 - sig)))).astype(BF16)

    width = out_ref.shape[1]
    n_look = cols_ref.shape[1]
    n_owner = out_ref.shape[0] // (3 * SLOTS)
    n_feat = w_ref.shape[0] // width
    grad_t = dot(w_ref[...], grad, 1, 1)
    emb_t = jnp.concatenate([grad_t[f * width : (f + 1) * width] for f in range(n_feat)], axis=1)
    factors = (looked_ref[1].astype(F32), looked_ref[0].astype(F32), None)
    parts = []
    for k in range(3):
        row_t = emb_t if factors[k] is None else emb_t * factors[k]
        high = row_t.astype(BF16)
        low = (row_t - high.astype(F32)).astype(BF16)
        onehot = hot(iota((n_owner * SLOTS, n_look), 0) == cols_ref[k : k + 1, :])
        sums = dot(onehot, jnp.concatenate([high, low], axis=0), 1, 1)
        sums = sums[:, :width] + sums[:, width:]
        parts.append(sums.reshape(n_owner, SLOTS, width))
    out_ref[...] = jnp.concatenate(parts, axis=1).reshape(n_owner * 3 * SLOTS, width).astype(BF16)


def owner_kernel(codes_ref, grads_ref, out_ref):
    n_src = codes_ref.shape[0]
    rows_dev, width = out_ref.shape[1:]
    codes = codes_ref[...]
    grads = grads_ref[...].astype(F32).reshape(n_src, 3 * SLOTS, width)
    for k in range(3):
        mine = grads[:, k * SLOTS : (k + 1) * SLOTS, :].reshape(n_src * SLOTS, width).astype(BF16)
        onehot = hot(iota((n_src * SLOTS, rows_dev), 1) == request_column(codes, k))
        out_ref[k] = dot(mine, onehot, 0, 0).T


def exchange(array, axis):
    return lax.all_to_all(array, axis, split_axis=0, concat_axis=0, tiled=True)


def body(owner, offset, tables, w_first, b_first, w_out, labels):
    n_rows = lax.axis_size("rows")
    n_grp = lax.axis_size("grp")
    n_b, n_feat = owner.shape[:2]
    rows_dev, width = tables.shape[1:]
    hidden = w_first.shape[1]
    n_look = n_b * n_feat
    shape = jax.ShapeDtypeStruct
    cols, asked, low = call(
        index_kernel,
        (
            shape((4, n_look), jnp.int32),
            shape((n_rows, LANES), jnp.int32),
            shape(tables.shape, BF16),
        ),
        spaces=[pltpu.VMEM, pltpu.HBM, pltpu.SMEM],
        vmem=VMEM_INDEX,
        scratch=(
            pltpu.VMEM(tables.shape, F32),
            pltpu.SemaphoreType.DMA,
        ),
    )(
        (owner * rows_dev + offset).transpose(1, 2, 0),
        tables,
        lax.axis_index("grp").astype(jnp.int32).reshape(1),
    )
    requests = exchange(asked, "rows")
    rows = call(fetch_kernel, shape((n_rows * 3 * SLOTS, width), BF16), n_in=2)(requests, low)
    rows = exchange(rows, "rows")
    pre, looked = call(
        forward_kernel,
        (shape((n_grp, n_b, hidden), BF16), shape((2, width, n_look), BF16)),
        n_in=3,
    )(rows, cols, w_first)
    pre = exchange(pre, "grp")
    share = n_b // n_grp
    sums, losses = call(
        backward_kernel,
        (shape((n_rows * 3 * SLOTS, width), BF16), shape((1, share), F32)),
        n_in=7,
    )(
        pre,
        b_first.reshape(1, hidden),
        w_out.reshape(1, hidden),
        labels.reshape(1, n_b),
        w_first,
        cols,
        looked,
    )
    sums = exchange(sums, "rows")
    table_grad = call(owner_kernel, shape((3, rows_dev, width), F32), n_in=2)(requests, sums)
    return table_grad, losses.reshape(share)


def solution(mesh):
    placed = (
        P("rows", "grp", None),
        P("rows", "grp", None),
        P("grp", "rows", None),
        P("grp", None),
        P(),
        P(),
        P("rows"),
    )
    return jax.shard_map(
        body,
        mesh=mesh,
        in_specs=placed,
        out_specs=(P("grp", "rows", None), P(("rows", "grp"))),
        check_vma=False,
    )
```

```python
import jax
import jax.numpy as jnp
from jax import lax
from jax.experimental import pallas as pl
from jax.experimental.pallas import tpu as pltpu
from jax.sharding import PartitionSpec as P

SLOTS = 8
LANES = 128
VMEM = 40 * 2**20
BF16 = jnp.bfloat16
F32 = jnp.float32


def dot(a, b, ca, cb):
    return lax.dot_general(a, b, (((ca,), (cb,)), ((), ())), preferred_element_type=F32)


def iota(shape, dim):
    return lax.broadcasted_iota(jnp.int32, shape, dim)


def one_hot(size, index):
    shape = (size, index.shape[1])
    same = lax.broadcasted_iota(jnp.int16, shape, 0) == index.astype(jnp.int16)
    return jnp.where(same, jnp.ones((), BF16), jnp.zeros((), BF16))


def call(kernel, out_shape, n_in=1, spaces=None, out=None, scratch=()):
    spaces = spaces or [pltpu.VMEM] * n_in
    return pl.pallas_call(
        kernel,
        out_shape=out_shape,
        in_specs=[pl.BlockSpec(memory_space=space) for space in spaces],
        scratch_shapes=scratch,
        **({} if out is None else {"out_specs": pl.BlockSpec(memory_space=out)}),
        compiler_params=pltpu.CompilerParams(vmem_limit_bytes=VMEM),
        cost_estimate=pl.CostEstimate(flops=2**28, bytes_accessed=2**20, transcendentals=0),
    )


def index_kernel(
    owner_hbm,
    offset_hbm,
    table_hbm,
    grp_ref,
    cols_ref,
    out_ref,
    table_ref,
    owner_ref,
    offset_ref,
    sems,
):
    copies = [
        pltpu.make_async_copy(owner_hbm, owner_ref, sems.at[0]),
        pltpu.make_async_copy(offset_hbm, offset_ref, sems.at[1]),
        pltpu.make_async_copy(table_hbm, table_ref, sems.at[2]),
    ]
    for copy in copies:
        copy.start()
    rows_dev = table_ref.shape[1]
    n_owner = out_ref.shape[0]
    n_look = cols_ref.shape[1]
    n_feat = owner_ref.shape[0]
    shape = (rows_dev, rows_dev)
    before = jnp.where(iota(shape, 1) < iota(shape, 0), 1.0, 0.0).astype(BF16)
    pairs = []
    copies[0].wait()
    copies[1].wait()
    for k in range(3):
        owner = jnp.concatenate([owner_ref[f, k : k + 1, :] for f in range(n_feat)], axis=1)
        offset = jnp.concatenate([offset_ref[f, k : k + 1, :] for f in range(n_feat)], axis=1)
        pairs.append((owner, offset, one_hot(n_owner, owner), one_hot(rows_dev, offset)))
    by_look = [owner_hot.T for _, _, owner_hot, _ in pairs]
    present = jnp.concatenate([dot(pairs[k][3], by_look[k], 1, 0) for k in range(3)], axis=1)
    rank = dot(before, jnp.minimum(present, 1.0).astype(BF16), 1, 0).astype(BF16)
    asked = []
    for k in range(3):
        owner, offset, owner_hot, offset_hot = pairs[k]
        at_owner = dot(rank[:, k * n_owner : (k + 1) * n_owner], offset_hot, 0, 0)
        slot = jnp.sum(owner_hot.astype(F32) * at_owner, axis=0, keepdims=True).astype(jnp.int32)
        cols_ref[k : k + 1, :] = owner * SLOTS + slot
        slot_hot = jnp.where(iota((SLOTS, n_look), 0) == slot, 1.0, 0.0)
        high = offset // 16
        low = (offset - high * 16).astype(F32)
        sides = [slot_hot * high.astype(F32), slot_hot * low, slot_hot]
        sums = dot(jnp.concatenate(sides, axis=0).astype(BF16), by_look[k], 1, 0)
        high, low, count = (sums[i * SLOTS : (i + 1) * SLOTS] for i in range(3))
        offset = jnp.floor((high * 16.0 + low) / jnp.maximum(count, 1.0) + 0.5)
        asked.append(jnp.where(count > 0.5, offset, -1.0))
    asked.append(jnp.full((LANES - 3 * SLOTS, n_owner), -1.0, F32))
    out_ref[...] = jnp.concatenate(asked, axis=0).T.astype(jnp.int32)
    cols_ref[3:4, :] = jnp.full((1, n_look), grp_ref[0], jnp.int32)
    copies[2].wait()


def fetch_kernel(codes_ref, table_ref, out_ref, asked_ref):
    n_src = codes_ref.shape[0]
    rows_dev, width = table_ref.shape[1:]
    n_ask = n_src * SLOTS
    code = codes_ref[...] + 1
    high = code // 16
    low = (code - high * 16).astype(F32).astype(BF16)
    high = high.astype(F32).astype(BF16)
    spread = one_hot(n_src, iota((1, n_ask), 1) // SLOTS)
    wide = dot(high, spread, 0, 0) * 16.0 + dot(low, spread, 0, 0)
    mine = iota((SLOTS, n_ask), 0) == iota((SLOTS, n_ask), 1) % SLOTS
    parts = []
    for k in range(3):
        asked = jnp.where(mine, wide[k * SLOTS : (k + 1) * SLOTS], 0.0)
        asked = jnp.sum(asked, axis=0, keepdims=True).astype(jnp.int32) - 1
        asked_ref[k : k + 1, :] = asked
        rows = dot(table_ref[k].astype(BF16), one_hot(rows_dev, asked), 0, 0).T
        parts.append(rows.reshape(n_src, SLOTS, width))
    rows = jnp.concatenate(parts, axis=1)
    out_ref[...] = rows.reshape(n_ask * 3, width).astype(BF16)


def forward_kernel(rows_ref, cols_ref, w_ref, pre_ref, looked_ref):
    width = rows_ref.shape[1]
    n_look = cols_ref.shape[1]
    n_owner = rows_ref.shape[0] // (3 * SLOTS)
    n_feat = w_ref.shape[0] // width
    rows = rows_ref[...].astype(F32).reshape(n_owner, 3 * SLOTS, width)
    looked = []
    for k in range(3):
        mine = rows[:, k * SLOTS : (k + 1) * SLOTS, :].reshape(n_owner * SLOTS, width).astype(BF16)
        onehot = one_hot(n_owner * SLOTS, cols_ref[k : k + 1, :])
        looked.append(dot(mine, onehot, 0, 0))
    looked_ref[0] = looked[0].T.astype(BF16)
    looked_ref[1] = looked[1].T.astype(BF16)
    emb = (looked[0] * looked[1] + looked[2]).astype(BF16)
    n_b = n_look // n_feat
    emb = jnp.concatenate([emb[:, f * n_b : (f + 1) * n_b] for f in range(n_feat)], axis=0)
    pre = dot(emb, w_ref[...], 0, 0).astype(BF16)
    for g in range(pre_ref.shape[0]):
        pre_ref[g] = pre


def backward_kernel(
    pre_ref, b_ref, w_out_ref, labels_ref, w_ref, cols_ref, looked_ref, out_ref, loss_ref
):
    n_grp, n_b, _ = pre_ref.shape
    pre = b_ref[...]
    for g in range(n_grp):
        pre = pre + pre_ref[g].astype(F32)
    w_out = w_out_ref[...]
    sig = jax.nn.sigmoid(pre)
    logits = jnp.sum(pre * sig * w_out, axis=1, keepdims=True)
    diagonal = iota((n_b, n_b), 0) == iota((n_b, n_b), 1)
    targets = jnp.sum(jnp.where(diagonal, labels_ref[...].astype(F32), 0.0), axis=1, keepdims=True)
    soft = jnp.maximum(logits, 0.0) + jnp.log1p(jnp.exp(-jnp.abs(logits)))
    losses = soft - targets * logits
    share = loss_ref.shape[1]
    mine = iota((n_b, share), 0) == iota((n_b, share), 1) + cols_ref[3:4, :share] * share
    loss_ref[...] = jnp.sum(jnp.where(mine, losses, 0.0), axis=0, keepdims=True)
    grad_logit = jax.nn.sigmoid(logits) - targets
    grad = (grad_logit * w_out * (sig * (1.0 + pre * (1.0 - sig)))).astype(BF16)

    width = out_ref.shape[1]
    n_look = cols_ref.shape[1]
    n_owner = out_ref.shape[0] // (3 * SLOTS)
    n_feat = w_ref.shape[0] // width
    grad_emb = dot(grad, w_ref[...], 1, 1)
    emb_t = jnp.concatenate([grad_emb[:, f * width : (f + 1) * width] for f in range(n_feat)], axis=0)
    factors = (looked_ref[1].astype(F32), looked_ref[0].astype(F32), None)
    parts = []
    for k in range(3):
        row_t = emb_t if factors[k] is None else emb_t * factors[k]
        high = row_t.astype(BF16)
        low = (row_t - high.astype(F32)).astype(BF16)
        onehot = one_hot(n_owner * SLOTS, cols_ref[k : k + 1, :])
        sums = dot(onehot, jnp.concatenate([high, low], axis=1), 1, 0)
        sums = sums[:, :width] + sums[:, width:]
        parts.append(sums.reshape(n_owner, SLOTS, width))
    out_ref[...] = jnp.concatenate(parts, axis=1).reshape(n_owner * 3 * SLOTS, width).astype(BF16)


def owner_kernel(asked_ref, grads_ref, out_hbm, out_ref, sems):
    n_ask = asked_ref.shape[1]
    rows_dev, width = out_ref.shape[1:]
    grads = grads_ref[...].astype(F32).reshape(n_ask // SLOTS, 3 * SLOTS, width)
    copies = []
    for k in range(3):
        mine = grads[:, k * SLOTS : (k + 1) * SLOTS, :].reshape(n_ask, width).astype(BF16)
        out_ref[k] = dot(one_hot(rows_dev, asked_ref[k : k + 1, :]), mine, 1, 0)
        copies.append(pltpu.make_async_copy(out_ref.at[k], out_hbm.at[k], sems.at[k]))
        copies[k].start()
    for copy in copies:
        copy.wait()


def exchange(array, axis):
    return lax.all_to_all(array, axis, split_axis=0, concat_axis=0, tiled=True)


def body(owner, offset, tables, w_first, b_first, w_out, labels):
    n_rows = lax.axis_size("rows")
    n_grp = lax.axis_size("grp")
    n_b, n_feat = owner.shape[:2]
    rows_dev, width = tables.shape[1:]
    hidden = w_first.shape[1]
    n_look = n_b * n_feat
    shape = jax.ShapeDtypeStruct
    cols, asked, low = call(
        index_kernel,
        (
            shape((4, n_look), jnp.int32),
            shape((n_rows, LANES), jnp.int32),
            shape(tables.shape, F32),
        ),
        spaces=[pltpu.HBM] * 3 + [pltpu.SMEM],
        scratch=(
            pltpu.VMEM((n_feat, 3, n_b), jnp.int32),
            pltpu.VMEM((n_feat, 3, n_b), jnp.int32),
            pltpu.SemaphoreType.DMA((3,)),
        ),
    )(
        pltpu.with_memory_space_constraint(owner.transpose(1, 2, 0), pltpu.HBM),
        pltpu.with_memory_space_constraint(offset.transpose(1, 2, 0), pltpu.HBM),
        pltpu.with_memory_space_constraint(tables, pltpu.HBM),
        lax.axis_index("grp").astype(jnp.int32).reshape(1),
    )
    requests = exchange(asked, "rows")
    rows, asked = call(
        fetch_kernel,
        (
            shape((n_rows * 3 * SLOTS, width), BF16),
            shape((3, n_rows * SLOTS), jnp.int32),
        ),
        n_in=2,
    )(requests, low)
    rows = exchange(rows, "rows")
    pre, looked = call(
        forward_kernel,
        (shape((n_grp, n_b, hidden), BF16), shape((2, n_look, width), BF16)),
        n_in=3,
    )(rows, cols, w_first)
    pre = exchange(pre, "grp")
    share = n_b // n_grp
    sums, losses = call(
        backward_kernel,
        (shape((n_rows * 3 * SLOTS, width), BF16), shape((1, share), F32)),
        n_in=7,
    )(
        pre,
        b_first.reshape(1, hidden),
        w_out.reshape(1, hidden),
        labels.reshape(1, n_b),
        w_first,
        cols,
        looked,
    )
    sums = exchange(sums, "rows")
    table_grad = call(
        owner_kernel,
        shape((3, rows_dev, width), F32),
        n_in=2,
        out=pltpu.HBM,
        scratch=(pltpu.VMEM((3, rows_dev, width), F32), pltpu.SemaphoreType.DMA((3,))),
    )(asked, sums)
    return table_grad, losses.reshape(share)


def solution(mesh):
    placed = (
        P("rows", "grp", None),
        P("rows", "grp", None),
        P("grp", "rows", None),
        P("grp", None),
        P(),
        P(),
        P("rows"),
    )
    return jax.shard_map(
        body,
        mesh=mesh,
        in_specs=placed,
        out_specs=(P("grp", "rows", None), P(("rows", "grp"))),
        check_vma=False,
    )
```

```python
import jax
import jax.numpy as jnp
from jax import lax
from jax.experimental import pallas as pl
from jax.experimental.pallas import tpu as pltpu
from jax.sharding import PartitionSpec as P

SLOTS = 8
LANES = 128
VMEM = 40 * 2**20
BF16 = jnp.bfloat16
F32 = jnp.float32


def dot(a, b, ca, cb):
    return lax.dot_general(a, b, (((ca,), (cb,)), ((), ())), preferred_element_type=F32)


def iota(shape, dim):
    return lax.broadcasted_iota(jnp.int32, shape, dim)


def one_hot(size, index):
    shape = (size, index.shape[1])
    same = lax.broadcasted_iota(jnp.int16, shape, 0) == index.astype(jnp.int16)
    return jnp.where(same, jnp.ones((), BF16), jnp.zeros((), BF16))


def call(kernel, out_shape, n_in=1, spaces=None, out=None, scratch=()):
    spaces = spaces or [pltpu.VMEM] * n_in
    return pl.pallas_call(
        kernel,
        out_shape=out_shape,
        in_specs=[pl.BlockSpec(memory_space=space) for space in spaces],
        scratch_shapes=scratch,
        **({} if out is None else {"out_specs": pl.BlockSpec(memory_space=out)}),
        compiler_params=pltpu.CompilerParams(vmem_limit_bytes=VMEM),
        cost_estimate=pl.CostEstimate(flops=2**28, bytes_accessed=2**20, transcendentals=0),
    )


def index_kernel(
    owner_hbm,
    offset_hbm,
    table_hbm,
    grp_ref,
    out_ref,
    keys_ref,
    rank_ref,
    table_ref,
    owner_ref,
    offset_ref,
    sems,
):
    copies = [
        pltpu.make_async_copy(owner_hbm, owner_ref, sems.at[0]),
        pltpu.make_async_copy(offset_hbm, offset_ref, sems.at[1]),
        pltpu.make_async_copy(table_hbm, table_ref, sems.at[2]),
    ]
    for copy in copies:
        copy.start()
    rows_dev = table_ref.shape[1]
    n_owner = out_ref.shape[0]
    n_look = keys_ref.shape[1]
    n_feat = owner_ref.shape[0]
    shape = (rows_dev, rows_dev)
    before = jnp.where(iota(shape, 1) < iota(shape, 0), 1.0, 0.0).astype(BF16)
    pairs = []
    copies[0].wait()
    copies[1].wait()
    for k in range(3):
        owner = jnp.concatenate([owner_ref[f, k : k + 1, :] for f in range(n_feat)], axis=1)
        offset = jnp.concatenate([offset_ref[f, k : k + 1, :] for f in range(n_feat)], axis=1)
        pairs.append((owner, offset, one_hot(n_owner, owner), one_hot(rows_dev, offset)))
    by_look = [owner_hot.T for _, _, owner_hot, _ in pairs]
    present = jnp.concatenate([dot(pairs[k][3], by_look[k], 1, 0) for k in range(3)], axis=1)
    rank = dot(before, jnp.minimum(present, 1.0).astype(BF16), 1, 0).astype(BF16)
    rank_ref[...] = rank
    asked = []
    numbers = lax.broadcasted_iota(jnp.int16, (rows_dev, n_owner), 0) + jnp.int16(1)
    for k in range(3):
        keys_ref[k : k + 1, :] = pairs[k][0]
        keys_ref[k + 3 : k + 4, :] = pairs[k][1]
        mine = slice(k * n_owner, (k + 1) * n_owner)
        place = jnp.where(present[:, mine] > 0.5, rank[:, mine].astype(F32), -1.0)
        place = place.astype(jnp.int32).astype(jnp.int16)
        for s in range(SLOTS):
            found = jnp.where(place == jnp.int16(s), numbers, jnp.int16(0))
            while found.shape[0] > 16:
                half = found.shape[0] // 2
                found = found[:half] + found[half:]
            found = jnp.sum(found.astype(jnp.int32).astype(F32), axis=0, keepdims=True)
            asked.append(found - 1.0)
    asked.append(jnp.full((LANES - 3 * SLOTS, n_owner), -1.0, F32))
    out_ref[...] = jnp.concatenate(asked, axis=0).T.astype(jnp.int32)
    keys_ref[6:7, :] = jnp.full((1, n_look), grp_ref[0], jnp.int32)
    copies[2].wait()


def prepare_kernel(keys_ref, rank_ref, w_ref, cols_ref, wt_ref):
    rows_dev = rank_ref.shape[0]
    n_owner = rank_ref.shape[1] // 3
    for k in range(3):
        owner = keys_ref[k : k + 1, :]
        offset_hot = one_hot(rows_dev, keys_ref[k + 3 : k + 4, :])
        at_owner = dot(rank_ref[:, k * n_owner : (k + 1) * n_owner], offset_hot, 0, 0)
        slot = jnp.sum(one_hot(n_owner, owner).astype(F32) * at_owner, axis=0, keepdims=True)
        cols_ref[k : k + 1, :] = owner * SLOTS + slot.astype(jnp.int32)
    cols_ref[3:4, :] = keys_ref[6:7, :]
    wt_ref[...] = w_ref[...].T


def fetch_kernel(codes_ref, table_ref, out_ref, asked_ref):
    n_src = codes_ref.shape[0]
    rows_dev, width = table_ref.shape[1:]
    n_ask = n_src * SLOTS
    code = codes_ref[...] + 1
    high = code // 16
    low = (code - high * 16).astype(F32).astype(BF16)
    high = high.astype(F32).astype(BF16)
    spread = one_hot(n_src, iota((1, n_ask), 1) // SLOTS)
    wide = dot(high, spread, 0, 0) * 16.0 + dot(low, spread, 0, 0)
    mine = iota((SLOTS, n_ask), 0) == iota((SLOTS, n_ask), 1) % SLOTS
    parts = []
    for k in range(3):
        asked = jnp.where(mine, wide[k * SLOTS : (k + 1) * SLOTS], 0.0)
        asked = jnp.sum(asked, axis=0, keepdims=True).astype(jnp.int32) - 1
        asked_ref[k : k + 1, :] = asked
        rows = dot(table_ref[k].astype(BF16), one_hot(rows_dev, asked), 0, 0).T
        parts.append(rows.reshape(n_src, SLOTS, width))
    rows = jnp.concatenate(parts, axis=1)
    out_ref[...] = rows.reshape(n_ask * 3, width).astype(BF16)


def forward_kernel(rows_ref, cols_ref, w_ref, pre_ref, looked_ref):
    width = rows_ref.shape[1]
    n_look = cols_ref.shape[1]
    n_owner = rows_ref.shape[0] // (3 * SLOTS)
    n_feat = w_ref.shape[0] // width
    rows = rows_ref[...].astype(F32).reshape(n_owner, 3 * SLOTS, width)
    looked = []
    for k in range(3):
        mine = rows[:, k * SLOTS : (k + 1) * SLOTS, :].reshape(n_owner * SLOTS, width).astype(BF16)
        onehot = one_hot(n_owner * SLOTS, cols_ref[k : k + 1, :])
        looked.append(dot(mine, onehot, 0, 0))
    looked_ref[0] = looked[0].T.astype(BF16)
    looked_ref[1] = looked[1].T.astype(BF16)
    emb = (looked[0] * looked[1] + looked[2]).astype(BF16)
    n_b = n_look // n_feat
    emb = jnp.concatenate([emb[:, f * n_b : (f + 1) * n_b] for f in range(n_feat)], axis=0)
    pre = dot(emb, w_ref[...], 0, 0).astype(BF16)
    for g in range(pre_ref.shape[0]):
        pre_ref[g] = pre


def backward_kernel(
    pre_ref, b_ref, w_out_ref, labels_ref, w_ref, cols_ref, looked_ref, out_ref, loss_ref
):
    n_grp, n_b, _ = pre_ref.shape
    pre = b_ref[...]
    for g in range(n_grp):
        pre = pre + pre_ref[g].astype(F32)
    w_out = w_out_ref[...]
    sig = jax.nn.sigmoid(pre)
    logits = jnp.sum(pre * sig * w_out, axis=1, keepdims=True)
    diagonal = iota((n_b, n_b), 0) == iota((n_b, n_b), 1)
    targets = jnp.sum(jnp.where(diagonal, labels_ref[...].astype(F32), 0.0), axis=1, keepdims=True)
    soft = jnp.maximum(logits, 0.0) + jnp.log1p(jnp.exp(-jnp.abs(logits)))
    losses = soft - targets * logits
    share = loss_ref.shape[1]
    mine = iota((n_b, share), 0) == iota((n_b, share), 1) + cols_ref[3:4, :share] * share
    loss_ref[...] = jnp.sum(jnp.where(mine, losses, 0.0), axis=0, keepdims=True)
    grad_logit = jax.nn.sigmoid(logits) - targets
    grad = (grad_logit * w_out * (sig * (1.0 + pre * (1.0 - sig)))).astype(BF16)

    width = out_ref.shape[1]
    n_look = cols_ref.shape[1]
    n_owner = out_ref.shape[0] // (3 * SLOTS)
    n_feat = w_ref.shape[1] // width
    grad_emb = dot(grad, w_ref[...], 1, 0)
    emb_t = jnp.concatenate([grad_emb[:, f * width : (f + 1) * width] for f in range(n_feat)], axis=0)
    factors = (looked_ref[1].astype(F32), looked_ref[0].astype(F32), None)
    parts = []
    for k in range(3):
        row_t = emb_t if factors[k] is None else emb_t * factors[k]
        high = row_t.astype(BF16)
        low = (row_t - high.astype(F32)).astype(BF16)
        onehot = one_hot(n_owner * SLOTS, cols_ref[k : k + 1, :])
        sums = dot(onehot, jnp.concatenate([high, low], axis=1), 1, 0)
        sums = sums[:, :width] + sums[:, width:]
        parts.append(sums.reshape(n_owner, SLOTS, width))
    out_ref[...] = jnp.concatenate(parts, axis=1).reshape(n_owner * 3 * SLOTS, width).astype(BF16)


def owner_kernel(asked_ref, grads_ref, out_hbm, out_ref, sems):
    n_ask = asked_ref.shape[1]
    rows_dev, width = out_ref.shape[1:]
    grads = grads_ref[...].astype(F32).reshape(n_ask // SLOTS, 3 * SLOTS, width)
    copies = []
    for k in range(3):
        mine = grads[:, k * SLOTS : (k + 1) * SLOTS, :].reshape(n_ask, width).astype(BF16)
        for h in range(2):
            half = pl.ds(h * rows_dev // 2, rows_dev // 2)
            out_ref[k, half] = dot(one_hot(rows_dev // 2, asked_ref[k : k + 1, :] - h * rows_dev // 2), mine, 1, 0)
            copies.append(pltpu.make_async_copy(out_ref.at[k, half], out_hbm.at[k, half], sems.at[2 * k + h]))
            copies[-1].start()
    for copy in copies:
        copy.wait()


def exchange(array, axis):
    return lax.all_to_all(array, axis, split_axis=0, concat_axis=0, tiled=True)


def body(owner, offset, tables, w_first, b_first, w_out, labels):
    n_rows = lax.axis_size("rows")
    n_grp = lax.axis_size("grp")
    n_b, n_feat = owner.shape[:2]
    rows_dev, width = tables.shape[1:]
    hidden = w_first.shape[1]
    n_look = n_b * n_feat
    shape = jax.ShapeDtypeStruct
    asked, keys, rank, table = call(
        index_kernel,
        (
            shape((n_rows, LANES), jnp.int32),
            shape((7, n_look), jnp.int32),
            shape((rows_dev, 3 * n_rows), BF16),
            shape(tables.shape, F32),
        ),
        spaces=[pltpu.HBM] * 3 + [pltpu.SMEM],
        scratch=(
            pltpu.VMEM((n_feat, 3, n_b), jnp.int32),
            pltpu.VMEM((n_feat, 3, n_b), jnp.int32),
            pltpu.SemaphoreType.DMA((3,)),
        ),
    )(
        pltpu.with_memory_space_constraint(owner.transpose(1, 2, 0), pltpu.HBM),
        pltpu.with_memory_space_constraint(offset.transpose(1, 2, 0), pltpu.HBM),
        pltpu.with_memory_space_constraint(tables, pltpu.HBM),
        lax.axis_index("grp").astype(jnp.int32).reshape(1),
    )
    cols, w_turned = call(
        prepare_kernel,
        (shape((4, n_look), jnp.int32), shape((hidden, n_feat * width), BF16)),
        n_in=3,
    )(keys, rank, w_first)
    requests = exchange(asked, "rows")
    rows, asked = call(
        fetch_kernel,
        (
            shape((n_rows * 3 * SLOTS, width), BF16),
            shape((3, n_rows * SLOTS), jnp.int32),
        ),
        n_in=2,
    )(requests, table)
    rows = exchange(rows, "rows")
    pre, looked = call(
        forward_kernel,
        (shape((n_grp, n_b, hidden), BF16), shape((2, n_look, width), BF16)),
        n_in=3,
    )(rows, cols, w_first)
    pre = exchange(pre, "grp")
    share = n_b // n_grp
    sums, losses = call(
        backward_kernel,
        (shape((n_rows * 3 * SLOTS, width), BF16), shape((1, share), F32)),
        n_in=7,
    )(
        pre,
        b_first.reshape(1, hidden),
        w_out.reshape(1, hidden),
        labels.reshape(1, n_b),
        w_turned,
        cols,
        looked,
    )
    sums = exchange(sums, "rows")
    table_grad = call(
        owner_kernel,
        shape((3, rows_dev, width), F32),
        n_in=2,
        out=pltpu.HBM,
        scratch=(pltpu.VMEM((3, rows_dev, width), F32), pltpu.SemaphoreType.DMA((6,))),
    )(asked, sums)
    return table_grad, losses.reshape(share)


def solution(mesh):
    placed = (
        P("rows", "grp", None),
        P("rows", "grp", None),
        P("grp", "rows", None),
        P("grp", None),
        P(),
        P(),
        P("rows"),
    )
    return jax.shard_map(
        body,
        mesh=mesh,
        in_specs=placed,
        out_specs=(P("grp", "rows", None), P(("rows", "grp"))),
        check_vma=False,
    )
```

```python
import jax
import jax.numpy as jnp
from jax import lax
from jax.experimental import pallas as pl
from jax.experimental.pallas import tpu as pltpu
from jax.sharding import PartitionSpec as P

SLOTS = 8
LANES = 128
VMEM = 40 * 2**20
BF16 = jnp.bfloat16
F32 = jnp.float32


def dot(a, b, ca, cb):
    return lax.dot_general(a, b, (((ca,), (cb,)), ((), ())), preferred_element_type=F32)


def iota(shape, dim):
    return lax.broadcasted_iota(jnp.int32, shape, dim)


def one_hot(size, index):
    shape = (size, index.shape[1])
    same = lax.broadcasted_iota(jnp.int16, shape, 0) == index.astype(jnp.int16)
    return jnp.where(same, jnp.ones((), BF16), jnp.zeros((), BF16))


def call(kernel, out_shape, n_in=1, spaces=None, out=None, scratch=()):
    spaces = spaces or [pltpu.VMEM] * n_in
    return pl.pallas_call(
        kernel,
        out_shape=out_shape,
        in_specs=[pl.BlockSpec(memory_space=space) for space in spaces],
        scratch_shapes=scratch,
        **({} if out is None else {"out_specs": pl.BlockSpec(memory_space=out)}),
        compiler_params=pltpu.CompilerParams(vmem_limit_bytes=VMEM),
        cost_estimate=pl.CostEstimate(flops=2**28, bytes_accessed=2**20, transcendentals=0),
    )


def index_kernel(
    owner_hbm,
    offset_hbm,
    table_hbm,
    grp_ref,
    out_ref,
    keys_ref,
    rank_ref,
    table_ref,
    owner_ref,
    offset_ref,
    sems,
):
    copies = [
        pltpu.make_async_copy(owner_hbm, owner_ref, sems.at[0]),
        pltpu.make_async_copy(offset_hbm, offset_ref, sems.at[1]),
        pltpu.make_async_copy(table_hbm, table_ref, sems.at[2]),
    ]
    for copy in copies:
        copy.start()
    rows_dev = table_ref.shape[1]
    n_owner = out_ref.shape[0]
    n_look = keys_ref.shape[1]
    n_feat = owner_ref.shape[0]
    shape = (rows_dev, rows_dev)
    before = jnp.where(iota(shape, 1) < iota(shape, 0), 1.0, 0.0).astype(BF16)
    pairs = []
    copies[0].wait()
    copies[1].wait()
    for k in range(3):
        owner = jnp.concatenate([owner_ref[f, k : k + 1, :] for f in range(n_feat)], axis=1)
        offset = jnp.concatenate([offset_ref[f, k : k + 1, :] for f in range(n_feat)], axis=1)
        pairs.append((owner, offset, one_hot(n_owner, owner), one_hot(rows_dev, offset)))
    by_look = [owner_hot.T for _, _, owner_hot, _ in pairs]
    present = jnp.concatenate([dot(pairs[k][3], by_look[k], 1, 0) for k in range(3)], axis=1)
    rank = dot(before, jnp.minimum(present, 1.0).astype(BF16), 1, 0).astype(BF16)
    rank_ref[...] = rank
    asked = []
    numbers = lax.broadcasted_iota(jnp.int16, (rows_dev, n_owner), 0) + jnp.int16(1)
    for k in range(3):
        keys_ref[k : k + 1, :] = pairs[k][0]
        keys_ref[k + 3 : k + 4, :] = pairs[k][1]
        mine = slice(k * n_owner, (k + 1) * n_owner)
        place = jnp.where(present[:, mine] > 0.5, rank[:, mine].astype(F32), -1.0)
        place = place.astype(jnp.int32).astype(jnp.int16)
        for s in range(SLOTS):
            found = jnp.where(place == jnp.int16(s), numbers, jnp.int16(0))
            while found.shape[0] > 16:
                half = found.shape[0] // 2
                found = found[:half] + found[half:]
            found = jnp.sum(found.astype(jnp.int32).astype(F32), axis=0, keepdims=True)
            asked.append(found - 1.0)
    asked.append(jnp.full((LANES - 3 * SLOTS, n_owner), -1.0, F32))
    out_ref[...] = jnp.concatenate(asked, axis=0).T.astype(jnp.int32)
    keys_ref[6:7, :] = jnp.full((1, n_look), grp_ref[0], jnp.int32)
    copies[2].wait()


def fetch_kernel(codes_ref, table_ref, keys_ref, rank_ref, out_ref, asked_ref, cols_ref):
    n_src = codes_ref.shape[0]
    rows_dev, width = table_ref.shape[1:]
    n_ask = n_src * SLOTS
    code = codes_ref[...] + 1
    high = code // 16
    low = (code - high * 16).astype(F32).astype(BF16)
    high = high.astype(F32).astype(BF16)
    spread = one_hot(n_src, iota((1, n_ask), 1) // SLOTS)
    wide = dot(high, spread, 0, 0) * 16.0 + dot(low, spread, 0, 0)
    mine = iota((SLOTS, n_ask), 0) == iota((SLOTS, n_ask), 1) % SLOTS
    parts = []
    for k in range(3):
        owner = keys_ref[k : k + 1, :]
        offset_hot = one_hot(rows_dev, keys_ref[k + 3 : k + 4, :])
        at_owner = dot(rank_ref[:, k * n_src : (k + 1) * n_src], offset_hot, 0, 0)
        slot = jnp.sum(one_hot(n_src, owner).astype(F32) * at_owner, axis=0, keepdims=True)
        cols_ref[k : k + 1, :] = owner * SLOTS + slot.astype(jnp.int32)
        asked = jnp.where(mine, wide[k * SLOTS : (k + 1) * SLOTS], 0.0)
        asked = jnp.sum(asked, axis=0, keepdims=True).astype(jnp.int32) - 1
        asked_ref[k : k + 1, :] = asked
        rows = dot(table_ref[k].astype(BF16), one_hot(rows_dev, asked), 0, 0).T
        parts.append(rows.reshape(n_src, SLOTS, width))
    cols_ref[3:4, :] = keys_ref[6:7, :]
    rows = jnp.concatenate(parts, axis=1)
    out_ref[...] = rows.reshape(n_ask * 3, width).astype(BF16)


def forward_kernel(rows_ref, cols_ref, w_ref, pre_ref, looked_ref, turned_ref):
    width = rows_ref.shape[1]
    n_look = cols_ref.shape[1]
    n_owner = rows_ref.shape[0] // (3 * SLOTS)
    n_feat = w_ref.shape[0] // width
    rows = rows_ref[...].astype(F32).reshape(n_owner, 3 * SLOTS, width)
    looked = []
    for k in range(3):
        mine = rows[:, k * SLOTS : (k + 1) * SLOTS, :].reshape(n_owner * SLOTS, width).astype(BF16)
        onehot = one_hot(n_owner * SLOTS, cols_ref[k : k + 1, :])
        looked.append(dot(mine, onehot, 0, 0))
    looked_ref[0] = looked[0].T.astype(BF16)
    looked_ref[1] = looked[1].T.astype(BF16)
    emb = (looked[0] * looked[1] + looked[2]).astype(BF16)
    n_b = n_look // n_feat
    emb = jnp.concatenate([emb[:, f * n_b : (f + 1) * n_b] for f in range(n_feat)], axis=0)
    turned_ref[...] = w_ref[...].T
    pre = dot(emb, w_ref[...], 0, 0).astype(BF16)
    for g in range(pre_ref.shape[0]):
        pre_ref[g] = pre


def backward_kernel(
    pre_ref, b_ref, w_out_ref, labels_ref, w_ref, cols_ref, looked_ref, out_ref, loss_ref
):
    n_grp, n_b, _ = pre_ref.shape
    pre = b_ref[...]
    for g in range(n_grp):
        pre = pre + pre_ref[g].astype(F32)
    w_out = w_out_ref[...]
    sig = jax.nn.sigmoid(pre)
    logits = jnp.sum(pre * sig * w_out, axis=1, keepdims=True)
    diagonal = iota((n_b, n_b), 0) == iota((n_b, n_b), 1)
    targets = jnp.sum(jnp.where(diagonal, labels_ref[...].astype(F32), 0.0), axis=1, keepdims=True)
    soft = jnp.maximum(logits, 0.0) + jnp.log1p(jnp.exp(-jnp.abs(logits)))
    losses = soft - targets * logits
    share = loss_ref.shape[1]
    mine = iota((n_b, share), 0) == iota((n_b, share), 1) + cols_ref[3:4, :share] * share
    loss_ref[...] = jnp.sum(jnp.where(mine, losses, 0.0), axis=0, keepdims=True)
    grad_logit = jax.nn.sigmoid(logits) - targets
    grad = (grad_logit * w_out * (sig * (1.0 + pre * (1.0 - sig)))).astype(BF16)

    width = out_ref.shape[1]
    n_look = cols_ref.shape[1]
    n_owner = out_ref.shape[0] // (3 * SLOTS)
    n_feat = w_ref.shape[1] // width
    grad_emb = dot(grad, w_ref[...], 1, 0)
    emb_t = jnp.concatenate([grad_emb[:, f * width : (f + 1) * width] for f in range(n_feat)], axis=0)
    factors = (looked_ref[1].astype(F32), looked_ref[0].astype(F32), None)
    parts = []
    for k in range(3):
        row_t = emb_t if factors[k] is None else emb_t * factors[k]
        high = row_t.astype(BF16)
        low = (row_t - high.astype(F32)).astype(BF16)
        onehot = one_hot(n_owner * SLOTS, cols_ref[k : k + 1, :])
        sums = dot(onehot, jnp.concatenate([high, low], axis=1), 1, 0)
        sums = sums[:, :width] + sums[:, width:]
        parts.append(sums.reshape(n_owner, SLOTS, width))
    out_ref[...] = jnp.concatenate(parts, axis=1).reshape(n_owner * 3 * SLOTS, width).astype(BF16)


def owner_kernel(asked_ref, grads_ref, out_hbm, out_ref, sems):
    n_ask = asked_ref.shape[1]
    rows_dev, width = out_ref.shape[1:]
    grads = grads_ref[...].astype(F32).reshape(n_ask // SLOTS, 3 * SLOTS, width)
    copies = []
    for k in range(3):
        mine = grads[:, k * SLOTS : (k + 1) * SLOTS, :].reshape(n_ask, width).astype(BF16)
        for h in range(2):
            half = pl.ds(h * rows_dev // 2, rows_dev // 2)
            out_ref[k, half] = dot(one_hot(rows_dev // 2, asked_ref[k : k + 1, :] - h * rows_dev // 2), mine, 1, 0)
            copies.append(pltpu.make_async_copy(out_ref.at[k, half], out_hbm.at[k, half], sems.at[2 * k + h]))
            copies[-1].start()
    for copy in copies:
        copy.wait()


def exchange(array, axis):
    return lax.all_to_all(array, axis, split_axis=0, concat_axis=0, tiled=True)


def body(owner, offset, tables, w_first, b_first, w_out, labels):
    n_rows = lax.axis_size("rows")
    n_grp = lax.axis_size("grp")
    n_b, n_feat = owner.shape[:2]
    rows_dev, width = tables.shape[1:]
    hidden = w_first.shape[1]
    n_look = n_b * n_feat
    shape = jax.ShapeDtypeStruct
    asked, keys, rank, table = call(
        index_kernel,
        (
            shape((n_rows, LANES), jnp.int32),
            shape((7, n_look), jnp.int32),
            shape((rows_dev, 3 * n_rows), BF16),
            shape(tables.shape, F32),
        ),
        spaces=[pltpu.HBM] * 3 + [pltpu.SMEM],
        scratch=(
            pltpu.VMEM((n_feat, 3, n_b), jnp.int32),
            pltpu.VMEM((n_feat, 3, n_b), jnp.int32),
            pltpu.SemaphoreType.DMA((3,)),
        ),
    )(
        pltpu.with_memory_space_constraint(owner.transpose(1, 2, 0), pltpu.HBM),
        pltpu.with_memory_space_constraint(offset.transpose(1, 2, 0), pltpu.HBM),
        pltpu.with_memory_space_constraint(tables, pltpu.HBM),
        lax.axis_index("grp").astype(jnp.int32).reshape(1),
    )
    requests = exchange(asked, "rows")
    rows, asked, cols = call(
        fetch_kernel,
        (
            shape((n_rows * 3 * SLOTS, width), BF16),
            shape((3, n_rows * SLOTS), jnp.int32),
            shape((4, n_look), jnp.int32),
        ),
        n_in=4,
    )(requests, table, keys, rank)
    rows = exchange(rows, "rows")
    pre, looked, w_turned = call(
        forward_kernel,
        (
            shape((n_grp, n_b, hidden), BF16),
            shape((2, n_look, width), BF16),
            shape((hidden, n_feat * width), BF16),
        ),
        n_in=3,
    )(rows, cols, w_first)
    pre = exchange(pre, "grp")
    share = n_b // n_grp
    sums, losses = call(
        backward_kernel,
        (shape((n_rows * 3 * SLOTS, width), BF16), shape((1, share), F32)),
        n_in=7,
    )(
        pre,
        b_first.reshape(1, hidden),
        w_out.reshape(1, hidden),
        labels.reshape(1, n_b),
        w_turned,
        cols,
        looked,
    )
    sums = exchange(sums, "rows")
    table_grad = call(
        owner_kernel,
        shape((3, rows_dev, width), F32),
        n_in=2,
        out=pltpu.HBM,
        scratch=(pltpu.VMEM((3, rows_dev, width), F32), pltpu.SemaphoreType.DMA((6,))),
    )(asked, sums)
    return table_grad, losses.reshape(share)


def solution(mesh):
    placed = (
        P("rows", "grp", None),
        P("rows", "grp", None),
        P("grp", "rows", None),
        P("grp", None),
        P(),
        P(),
        P("rows"),
    )
    return jax.shard_map(
        body,
        mesh=mesh,
        in_specs=placed,
        out_specs=(P("grp", "rows", None), P(("rows", "grp"))),
        check_vma=False,
    )
```

```python
import jax
import jax.numpy as jnp
from jax import lax
from jax.experimental import pallas as pl
from jax.experimental.pallas import tpu as pltpu
from jax.sharding import PartitionSpec as P

SLOTS = 8
LANES = 128
VMEM = 40 * 2**20
BF16 = jnp.bfloat16
F32 = jnp.float32


def dot(a, b, ca, cb):
    return lax.dot_general(a, b, (((ca,), (cb,)), ((), ())), preferred_element_type=F32)


def iota(shape, dim):
    return lax.broadcasted_iota(jnp.int32, shape, dim)


def one_hot(size, index):
    shape = (size, index.shape[1])
    same = lax.broadcasted_iota(jnp.int16, shape, 0) == index.astype(jnp.int16)
    return jnp.where(same, jnp.ones((), BF16), jnp.zeros((), BF16))


def call(kernel, out_shape, n_in=1, spaces=None, out=None, scratch=()):
    spaces = spaces or [pltpu.VMEM] * n_in
    return pl.pallas_call(
        kernel,
        out_shape=out_shape,
        in_specs=[pl.BlockSpec(memory_space=space) for space in spaces],
        scratch_shapes=scratch,
        **({} if out is None else {"out_specs": pl.BlockSpec(memory_space=out)}),
        compiler_params=pltpu.CompilerParams(vmem_limit_bytes=VMEM),
        cost_estimate=pl.CostEstimate(flops=2**28, bytes_accessed=2**20, transcendentals=0),
    )


def index_kernel(
    owner_hbm,
    offset_hbm,
    table_hbm,
    grp_ref,
    out_ref,
    keys_ref,
    rank_ref,
    table_ref,
    owner_ref,
    offset_ref,
    sems,
):
    copies = [
        pltpu.make_async_copy(owner_hbm, owner_ref, sems.at[0]),
        pltpu.make_async_copy(offset_hbm, offset_ref, sems.at[1]),
        pltpu.make_async_copy(table_hbm, table_ref, sems.at[2]),
    ]
    for copy in copies:
        copy.start()
    rows_dev = table_ref.shape[1]
    n_owner = out_ref.shape[0]
    n_look = keys_ref.shape[1]
    n_feat = owner_ref.shape[0]
    shape = (rows_dev, rows_dev)
    before = jnp.where(iota(shape, 1) < iota(shape, 0), 1.0, 0.0).astype(BF16)
    pairs = []
    copies[0].wait()
    copies[1].wait()
    for k in range(3):
        owner = jnp.concatenate([owner_ref[f, k : k + 1, :] for f in range(n_feat)], axis=1)
        offset = jnp.concatenate([offset_ref[f, k : k + 1, :] for f in range(n_feat)], axis=1)
        pairs.append((owner, offset, one_hot(n_owner, owner), one_hot(rows_dev, offset)))
    by_look = [owner_hot.T for _, _, owner_hot, _ in pairs]
    present = jnp.concatenate([dot(pairs[k][3], by_look[k], 1, 0) for k in range(3)], axis=1)
    rank = dot(before, jnp.minimum(present, 1.0).astype(BF16), 1, 0).astype(BF16)
    rank_ref[...] = rank
    asked = []
    numbers = lax.broadcasted_iota(jnp.int16, (rows_dev, n_owner), 0) + jnp.int16(1)
    for k in range(3):
        keys_ref[k : k + 1, :] = pairs[k][0]
        keys_ref[k + 3 : k + 4, :] = pairs[k][1]
        mine = slice(k * n_owner, (k + 1) * n_owner)
        place = jnp.where(present[:, mine] > 0.5, rank[:, mine].astype(F32), -1.0)
        place = place.astype(jnp.int32).astype(jnp.int16)
        for s in range(SLOTS):
            found = jnp.where(place == jnp.int16(s), numbers, jnp.int16(0))
            while found.shape[0] > 16:
                half = found.shape[0] // 2
                found = found[:half] + found[half:]
            found = jnp.sum(found.astype(jnp.int32).astype(F32), axis=0, keepdims=True)
            asked.append(found - 1.0)
    asked.append(jnp.full((LANES - 3 * SLOTS, n_owner), -1.0, F32))
    out_ref[...] = jnp.concatenate(asked, axis=0).T.astype(jnp.int32)
    keys_ref[6:7, :] = jnp.full((1, n_look), grp_ref[0], jnp.int32)
    copies[2].wait()


def fetch_kernel(codes_ref, table_ref, keys_ref, rank_ref, out_ref, asked_ref, cols_ref):
    n_src = codes_ref.shape[0]
    rows_dev, width = table_ref.shape[1:]
    n_ask = n_src * SLOTS
    code = codes_ref[...] + 1
    high = code // 16
    low = (code - high * 16).astype(F32).astype(BF16)
    high = high.astype(F32).astype(BF16)
    spread = one_hot(n_src, iota((1, n_ask), 1) // SLOTS)
    wide = dot(high, spread, 0, 0) * 16.0 + dot(low, spread, 0, 0)
    mine = iota((SLOTS, n_ask), 0) == iota((SLOTS, n_ask), 1) % SLOTS
    parts = []
    for k in range(3):
        owner = keys_ref[k : k + 1, :]
        offset_hot = one_hot(rows_dev, keys_ref[k + 3 : k + 4, :])
        at_owner = dot(rank_ref[:, k * n_src : (k + 1) * n_src], offset_hot, 0, 0)
        slot = jnp.sum(one_hot(n_src, owner).astype(F32) * at_owner, axis=0, keepdims=True)
        cols_ref[k : k + 1, :] = owner * SLOTS + slot.astype(jnp.int32)
        asked = jnp.where(mine, wide[k * SLOTS : (k + 1) * SLOTS], 0.0)
        asked = jnp.sum(asked, axis=0, keepdims=True).astype(jnp.int32) - 1
        asked_ref[k : k + 1, :] = asked
        rows = dot(table_ref[k].astype(BF16), one_hot(rows_dev, asked), 0, 0).T
        parts.append(rows.reshape(n_src, SLOTS, width))
    cols_ref[3:4, :] = keys_ref[6:7, :]
    rows = jnp.concatenate(parts, axis=1)
    out_ref[...] = rows.reshape(n_ask * 3, width).astype(BF16)


def forward_kernel(rows_ref, cols_ref, w_ref, pre_ref, looked_ref, turned_ref):
    width = rows_ref.shape[1]
    n_look = cols_ref.shape[1]
    n_owner = rows_ref.shape[0] // (3 * SLOTS)
    n_feat = w_ref.shape[0] // width
    rows = rows_ref[...].astype(F32).reshape(n_owner, 3 * SLOTS, width)
    looked = []
    for k in range(3):
        mine = rows[:, k * SLOTS : (k + 1) * SLOTS, :].reshape(n_owner * SLOTS, width).astype(BF16)
        onehot = one_hot(n_owner * SLOTS, cols_ref[k : k + 1, :])
        looked.append(dot(mine, onehot, 0, 0))
    looked_ref[0] = looked[0].T.astype(BF16)
    looked_ref[1] = looked[1].T.astype(BF16)
    emb = (looked[0] * looked[1] + looked[2]).astype(BF16)
    n_b = n_look // n_feat
    emb = jnp.concatenate([emb[:, f * n_b : (f + 1) * n_b] for f in range(n_feat)], axis=0)
    turned_ref[...] = w_ref[...].T
    pre = dot(emb, w_ref[...], 0, 0).astype(BF16)
    pre_ref[...] = pre


def head_kernel(pre_ref, b_ref, w_out_ref, labels_ref, cols_ref, grad_ref, loss_ref):
    n_grp, share, _ = pre_ref.shape
    n_b = labels_ref.shape[1]
    pre = b_ref[...]
    for g in range(n_grp):
        pre = pre + pre_ref[g].astype(F32)
    w_out = w_out_ref[...]
    sig = jax.nn.sigmoid(pre)
    logits = jnp.sum(pre * sig * w_out, axis=1, keepdims=True)
    mine = iota((share, n_b), 1) == iota((share, n_b), 0) + cols_ref[3:4, :n_b] * share
    targets = jnp.sum(jnp.where(mine, labels_ref[...].astype(F32), 0.0), axis=1, keepdims=True)
    soft = jnp.maximum(logits, 0.0) + jnp.log1p(jnp.exp(-jnp.abs(logits)))
    losses = soft - targets * logits
    diagonal = iota((share, share), 0) == iota((share, share), 1)
    loss_ref[...] = jnp.sum(jnp.where(diagonal, losses, 0.0), axis=0, keepdims=True)
    grad_logit = jax.nn.sigmoid(logits) - targets
    grad = (grad_logit * w_out * (sig * (1.0 + pre * (1.0 - sig)))).astype(BF16)
    for g in range(n_grp):
        grad_ref[g] = grad


def backward_kernel(grad_ref, w_ref, cols_ref, looked_ref, out_ref):
    grad = grad_ref[...]
    width = out_ref.shape[1]
    n_look = cols_ref.shape[1]
    n_owner = out_ref.shape[0] // (3 * SLOTS)
    n_feat = w_ref.shape[1] // width
    grad_emb = dot(grad, w_ref[...], 1, 0)
    emb_t = jnp.concatenate([grad_emb[:, f * width : (f + 1) * width] for f in range(n_feat)], axis=0)
    factors = (looked_ref[1].astype(F32), looked_ref[0].astype(F32), None)
    parts = []
    for k in range(3):
        row_t = emb_t if factors[k] is None else emb_t * factors[k]
        high = row_t.astype(BF16)
        low = (row_t - high.astype(F32)).astype(BF16)
        onehot = one_hot(n_owner * SLOTS, cols_ref[k : k + 1, :])
        sums = dot(onehot, jnp.concatenate([high, low], axis=1), 1, 0)
        sums = sums[:, :width] + sums[:, width:]
        parts.append(sums.reshape(n_owner, SLOTS, width))
    out_ref[...] = jnp.concatenate(parts, axis=1).reshape(n_owner * 3 * SLOTS, width).astype(BF16)


def owner_kernel(asked_ref, grads_ref, out_hbm, out_ref, sems):
    n_ask = asked_ref.shape[1]
    rows_dev, width = out_ref.shape[1:]
    grads = grads_ref[...].astype(F32).reshape(n_ask // SLOTS, 3 * SLOTS, width)
    copies = []
    for k in range(3):
        mine = grads[:, k * SLOTS : (k + 1) * SLOTS, :].reshape(n_ask, width).astype(BF16)
        for h in range(2):
            half = pl.ds(h * rows_dev // 2, rows_dev // 2)
            out_ref[k, half] = dot(one_hot(rows_dev // 2, asked_ref[k : k + 1, :] - h * rows_dev // 2), mine, 1, 0)
            copies.append(pltpu.make_async_copy(out_ref.at[k, half], out_hbm.at[k, half], sems.at[2 * k + h]))
            copies[-1].start()
    for copy in copies:
        copy.wait()


def exchange(array, axis):
    return lax.all_to_all(array, axis, split_axis=0, concat_axis=0, tiled=True)


def body(owner, offset, tables, w_first, b_first, w_out, labels):
    n_rows = lax.axis_size("rows")
    n_grp = lax.axis_size("grp")
    n_b, n_feat = owner.shape[:2]
    rows_dev, width = tables.shape[1:]
    hidden = w_first.shape[1]
    n_look = n_b * n_feat
    shape = jax.ShapeDtypeStruct
    asked, keys, rank, table = call(
        index_kernel,
        (
            shape((n_rows, LANES), jnp.int32),
            shape((7, n_look), jnp.int32),
            shape((rows_dev, 3 * n_rows), BF16),
            shape(tables.shape, F32),
        ),
        spaces=[pltpu.HBM] * 3 + [pltpu.SMEM],
        scratch=(
            pltpu.VMEM((n_feat, 3, n_b), jnp.int32),
            pltpu.VMEM((n_feat, 3, n_b), jnp.int32),
            pltpu.SemaphoreType.DMA((3,)),
        ),
    )(
        pltpu.with_memory_space_constraint(owner.transpose(1, 2, 0), pltpu.HBM),
        pltpu.with_memory_space_constraint(offset.transpose(1, 2, 0), pltpu.HBM),
        pltpu.with_memory_space_constraint(tables, pltpu.HBM),
        lax.axis_index("grp").astype(jnp.int32).reshape(1),
    )
    requests = exchange(asked, "rows")
    rows, asked, cols = call(
        fetch_kernel,
        (
            shape((n_rows * 3 * SLOTS, width), BF16),
            shape((3, n_rows * SLOTS), jnp.int32),
            shape((4, n_look), jnp.int32),
        ),
        n_in=4,
    )(requests, table, keys, rank)
    rows = exchange(rows, "rows")
    pre, looked, w_turned = call(
        forward_kernel,
        (
            shape((n_b, hidden), BF16),
            shape((2, n_look, width), BF16),
            shape((hidden, n_feat * width), BF16),
        ),
        n_in=3,
    )(rows, cols, w_first)
    share = n_b // n_grp
    pre = exchange(pre.reshape(n_grp, share, hidden), "grp")
    grad, losses = call(
        head_kernel,
        (shape((n_grp, share, hidden), BF16), shape((1, share), F32)),
        n_in=5,
    )(pre, b_first.reshape(1, hidden), w_out.reshape(1, hidden), labels.reshape(1, n_b), cols)
    grad = exchange(grad, "grp").reshape(n_b, hidden)
    sums = call(backward_kernel, shape((n_rows * 3 * SLOTS, width), BF16), n_in=4)(
        grad, w_turned, cols, looked
    )
    sums = exchange(sums, "rows")
    table_grad = call(
        owner_kernel,
        shape((3, rows_dev, width), F32),
        n_in=2,
        out=pltpu.HBM,
        scratch=(pltpu.VMEM((3, rows_dev, width), F32), pltpu.SemaphoreType.DMA((6,))),
    )(asked, sums)
    return table_grad, losses.reshape(share)


def solution(mesh):
    placed = (
        P("rows", "grp", None),
        P("rows", "grp", None),
        P("grp", "rows", None),
        P("grp", None),
        P(),
        P(),
        P("rows"),
    )
    return jax.shard_map(
        body,
        mesh=mesh,
        in_specs=placed,
        out_specs=(P("grp", "rows", None), P(("rows", "grp"))),
        check_vma=False,
    )
```

```python
import jax
import jax.numpy as jnp
from jax import lax
from jax.experimental import pallas as pl
from jax.experimental.pallas import tpu as pltpu
from jax.sharding import PartitionSpec as P

SLOTS = 8
LANES = 128
VMEM = 40 * 2**20
BF16 = jnp.bfloat16
F32 = jnp.float32


def dot(a, b, ca, cb):
    return lax.dot_general(a, b, (((ca,), (cb,)), ((), ())), preferred_element_type=F32)


def iota(shape, dim):
    return lax.broadcasted_iota(jnp.int32, shape, dim)


def one_hot(size, index):
    shape = (size, index.shape[1])
    same = lax.broadcasted_iota(jnp.int16, shape, 0) == index.astype(jnp.int16)
    return jnp.where(same, jnp.ones((), BF16), jnp.zeros((), BF16))


def call(kernel, out_shape, n_in=1, spaces=None, out=None, scratch=()):
    spaces = spaces or [pltpu.VMEM] * n_in
    return pl.pallas_call(
        kernel,
        out_shape=out_shape,
        in_specs=[pl.BlockSpec(memory_space=space) for space in spaces],
        scratch_shapes=scratch,
        **({} if out is None else {"out_specs": pl.BlockSpec(memory_space=out)}),
        compiler_params=pltpu.CompilerParams(vmem_limit_bytes=VMEM),
        cost_estimate=pl.CostEstimate(flops=2**28, bytes_accessed=2**20, transcendentals=0),
    )


def index_kernel(
    owner_hbm,
    offset_hbm,
    table_hbm,
    grp_ref,
    out_ref,
    keys_ref,
    rank_ref,
    table_ref,
    owner_ref,
    offset_ref,
    sems,
):
    copies = [
        pltpu.make_async_copy(owner_hbm, owner_ref, sems.at[0]),
        pltpu.make_async_copy(offset_hbm, offset_ref, sems.at[1]),
        pltpu.make_async_copy(table_hbm, table_ref, sems.at[2]),
    ]
    for copy in copies:
        copy.start()
    rows_dev = table_ref.shape[1]
    n_owner = out_ref.shape[0]
    n_look = keys_ref.shape[1]
    n_feat = owner_ref.shape[0]
    shape = (rows_dev, rows_dev)
    before = jnp.where(iota(shape, 1) < iota(shape, 0), 1.0, 0.0).astype(BF16)
    pairs = []
    copies[0].wait()
    copies[1].wait()
    for k in range(3):
        owner = jnp.concatenate([owner_ref[f, k : k + 1, :] for f in range(n_feat)], axis=1)
        offset = jnp.concatenate([offset_ref[f, k : k + 1, :] for f in range(n_feat)], axis=1)
        pairs.append((owner, offset, one_hot(n_owner, owner), one_hot(rows_dev, offset)))
    present = jnp.concatenate([dot(pairs[k][3], pairs[k][2], 1, 1) for k in range(3)], axis=1)
    rank = dot(before, jnp.minimum(present, 1.0).astype(BF16), 1, 0).astype(BF16)
    rank_ref[...] = rank
    asked = []
    numbers = lax.broadcasted_iota(jnp.int16, (rows_dev, n_owner), 0) + jnp.int16(1)
    for k in range(3):
        keys_ref[k : k + 1, :] = pairs[k][0]
        keys_ref[k + 3 : k + 4, :] = pairs[k][1]
        mine = slice(k * n_owner, (k + 1) * n_owner)
        place = jnp.where(present[:, mine] > 0.5, rank[:, mine].astype(F32), -1.0)
        place = place.astype(jnp.int32).astype(jnp.int16)
        for s in range(SLOTS):
            found = jnp.where(place == jnp.int16(s), numbers, jnp.int16(0))
            while found.shape[0] > 16:
                half = found.shape[0] // 2
                found = found[:half] + found[half:]
            found = jnp.sum(found.astype(jnp.int32).astype(F32), axis=0, keepdims=True)
            asked.append(found - 1.0)
    asked.append(jnp.full((LANES - 3 * SLOTS, n_owner), -1.0, F32))
    out_ref[...] = jnp.concatenate(asked, axis=0).T.astype(jnp.int32)
    keys_ref[6:7, :] = jnp.full((1, n_look), grp_ref[0], jnp.int32)
    copies[2].wait()


def fetch_kernel(codes_ref, table_ref, keys_ref, rank_ref, out_ref, asked_ref, cols_ref):
    n_src = codes_ref.shape[0]
    rows_dev, width = table_ref.shape[1:]
    n_ask = n_src * SLOTS
    code = codes_ref[...] + 1
    high = code // 16
    low = (code - high * 16).astype(F32).astype(BF16)
    high = high.astype(F32).astype(BF16)
    spread = one_hot(n_src, iota((1, n_ask), 1) // SLOTS)
    wide = dot(high, spread, 0, 0) * 16.0 + dot(low, spread, 0, 0)
    mine = iota((SLOTS, n_ask), 0) == iota((SLOTS, n_ask), 1) % SLOTS
    parts = []
    for k in range(3):
        owner = keys_ref[k : k + 1, :]
        offset_hot = one_hot(rows_dev, keys_ref[k + 3 : k + 4, :])
        at_owner = dot(rank_ref[:, k * n_src : (k + 1) * n_src], offset_hot, 0, 0)
        slot = jnp.sum(one_hot(n_src, owner).astype(F32) * at_owner, axis=0, keepdims=True)
        cols_ref[k : k + 1, :] = owner * SLOTS + slot.astype(jnp.int32)
        asked = jnp.where(mine, wide[k * SLOTS : (k + 1) * SLOTS], 0.0)
        asked = jnp.sum(asked, axis=0, keepdims=True).astype(jnp.int32) - 1
        asked_ref[k : k + 1, :] = asked
        rows = dot(table_ref[k].astype(BF16), one_hot(rows_dev, asked), 0, 0).astype(BF16).T.astype(F32)
        parts.append(rows.reshape(n_src, SLOTS, width))
    cols_ref[3:4, :] = keys_ref[6:7, :]
    rows = jnp.concatenate(parts, axis=1)
    out_ref[...] = rows.reshape(n_ask * 3, width).astype(BF16)


def forward_kernel(rows_ref, cols_ref, w_ref, pre_ref, looked_ref, turned_ref):
    width = rows_ref.shape[1]
    n_look = cols_ref.shape[1]
    n_owner = rows_ref.shape[0] // (3 * SLOTS)
    n_feat = w_ref.shape[0] // width
    rows = rows_ref[...].astype(F32).reshape(n_owner, 3 * SLOTS, width)
    looked = []
    for k in range(3):
        mine = rows[:, k * SLOTS : (k + 1) * SLOTS, :].reshape(n_owner * SLOTS, width).astype(BF16)
        onehot = one_hot(n_owner * SLOTS, cols_ref[k : k + 1, :])
        looked.append(dot(mine, onehot, 0, 0))
    looked_ref[0] = looked[0].astype(BF16).T
    looked_ref[1] = looked[1].astype(BF16).T
    emb = (looked[0] * looked[1] + looked[2]).astype(BF16)
    n_b = n_look // n_feat
    emb = jnp.concatenate([emb[:, f * n_b : (f + 1) * n_b] for f in range(n_feat)], axis=0)
    turned_ref[...] = w_ref[...].T
    pre = dot(emb, w_ref[...], 0, 0).astype(BF16)
    for g in range(pre_ref.shape[0]):
        pre_ref[g] = pre


def backward_kernel(
    pre_ref, b_ref, w_out_ref, labels_ref, w_ref, cols_ref, looked_ref, out_ref, loss_ref
):
    n_grp, n_b, _ = pre_ref.shape
    pre = b_ref[...]
    for g in range(n_grp):
        pre = pre + pre_ref[g].astype(F32)
    w_out = w_out_ref[...]
    sig = jax.nn.sigmoid(pre)
    logits = jnp.sum(pre * sig * w_out, axis=1, keepdims=True)
    diagonal = iota((n_b, n_b), 0) == iota((n_b, n_b), 1)
    targets = jnp.sum(jnp.where(diagonal, labels_ref[...].astype(F32), 0.0), axis=1, keepdims=True)
    soft = jnp.maximum(logits, 0.0) + jnp.log1p(jnp.exp(-jnp.abs(logits)))
    losses = soft - targets * logits
    share = loss_ref.shape[1]
    mine = iota((n_b, share), 0) == iota((n_b, share), 1) + cols_ref[3:4, :share] * share
    loss_ref[...] = jnp.sum(jnp.where(mine, losses, 0.0), axis=0, keepdims=True)
    grad_logit = jax.nn.sigmoid(logits) - targets
    grad = (grad_logit * w_out * (sig * (1.0 + pre * (1.0 - sig)))).astype(BF16)

    width = out_ref.shape[1]
    n_look = cols_ref.shape[1]
    n_owner = out_ref.shape[0] // (3 * SLOTS)
    n_feat = w_ref.shape[1] // width
    grad_emb = dot(grad, w_ref[...], 1, 0)
    emb_t = jnp.concatenate([grad_emb[:, f * width : (f + 1) * width] for f in range(n_feat)], axis=0)
    factors = (looked_ref[1].astype(F32), looked_ref[0].astype(F32), None)
    parts = []
    for k in range(3):
        row_t = emb_t if factors[k] is None else emb_t * factors[k]
        high = row_t.astype(BF16)
        low = (row_t - high.astype(F32)).astype(BF16)
        onehot = one_hot(n_owner * SLOTS, cols_ref[k : k + 1, :])
        sums = dot(onehot, jnp.concatenate([high, low], axis=1), 1, 0)
        sums = sums[:, :width] + sums[:, width:]
        parts.append(sums.reshape(n_owner, SLOTS, width))
    out_ref[...] = jnp.concatenate(parts, axis=1).reshape(n_owner * 3 * SLOTS, width).astype(BF16)


def owner_kernel(asked_ref, grads_ref, out_hbm, out_ref, sems):
    n_ask = asked_ref.shape[1]
    rows_dev, width = out_ref.shape[1:]
    grads = grads_ref[...].astype(F32).reshape(n_ask // SLOTS, 3 * SLOTS, width)
    copies = []
    for k in range(3):
        mine = grads[:, k * SLOTS : (k + 1) * SLOTS, :].reshape(n_ask, width).astype(BF16)
        for h in range(4):
            half = pl.ds(h * rows_dev // 4, rows_dev // 4)
            out_ref[k, half] = dot(one_hot(rows_dev // 4, asked_ref[k : k + 1, :] - h * rows_dev // 4), mine, 1, 0)
            copies.append(pltpu.make_async_copy(out_ref.at[k, half], out_hbm.at[k, half], sems.at[4 * k + h]))
            copies[-1].start()
    for copy in copies:
        copy.wait()


def exchange(array, axis):
    return lax.all_to_all(array, axis, split_axis=0, concat_axis=0, tiled=True)


def body(owner, offset, tables, w_first, b_first, w_out, labels):
    n_rows = lax.axis_size("rows")
    n_grp = lax.axis_size("grp")
    n_b, n_feat = owner.shape[:2]
    rows_dev, width = tables.shape[1:]
    hidden = w_first.shape[1]
    n_look = n_b * n_feat
    shape = jax.ShapeDtypeStruct
    asked, keys, rank, table = call(
        index_kernel,
        (
            shape((n_rows, LANES), jnp.int32),
            shape((7, n_look), jnp.int32),
            shape((rows_dev, 3 * n_rows), BF16),
            shape(tables.shape, F32),
        ),
        spaces=[pltpu.HBM] * 3 + [pltpu.SMEM],
        scratch=(
            pltpu.VMEM((n_feat, 3, n_b), jnp.int32),
            pltpu.VMEM((n_feat, 3, n_b), jnp.int32),
            pltpu.SemaphoreType.DMA((3,)),
        ),
    )(
        pltpu.with_memory_space_constraint(owner.transpose(1, 2, 0), pltpu.HBM),
        pltpu.with_memory_space_constraint(offset.transpose(1, 2, 0), pltpu.HBM),
        pltpu.with_memory_space_constraint(tables, pltpu.HBM),
        lax.axis_index("grp").astype(jnp.int32).reshape(1),
    )
    requests = exchange(asked, "rows")
    rows, asked, cols = call(
        fetch_kernel,
        (
            shape((n_rows * 3 * SLOTS, width), BF16),
            shape((3, n_rows * SLOTS), jnp.int32),
            shape((4, n_look), jnp.int32),
        ),
        n_in=4,
    )(requests, table, keys, rank)
    rows = exchange(rows, "rows")
    pre, looked, w_turned = call(
        forward_kernel,
        (
            shape((n_grp, n_b, hidden), BF16),
            shape((2, n_look, width), BF16),
            shape((hidden, n_feat * width), BF16),
        ),
        n_in=3,
    )(rows, cols, w_first)
    pre = exchange(pre, "grp")
    share = n_b // n_grp
    sums, losses = call(
        backward_kernel,
        (shape((n_rows * 3 * SLOTS, width), BF16), shape((1, share), F32)),
        n_in=7,
    )(
        pre,
        b_first.reshape(1, hidden),
        w_out.reshape(1, hidden),
        labels.reshape(1, n_b),
        w_turned,
        cols,
        looked,
    )
    sums = exchange(sums, "rows")
    table_grad = call(
        owner_kernel,
        shape((3, rows_dev, width), F32),
        n_in=2,
        out=pltpu.HBM,
        scratch=(pltpu.VMEM((3, rows_dev, width), F32), pltpu.SemaphoreType.DMA((12,))),
    )(asked, sums)
    return table_grad, losses.reshape(share)


def solution(mesh):
    placed = (
        P("rows", "grp", None),
        P("rows", "grp", None),
        P("grp", "rows", None),
        P("grp", None),
        P(),
        P(),
        P("rows"),
    )
    return jax.shard_map(
        body,
        mesh=mesh,
        in_specs=placed,
        out_specs=(P("grp", "rows", None), P(("rows", "grp"))),
        check_vma=False,
    )
```
